128 devices in a mesh: tm: 32 (over y, z, core), tp: 4 (over x).
Axes of the slice: x: 4, y: 4, z: 4, core: 2. Of those that a mesh axis runs over, the one named last changes fastest.
Arguments:
- latents: bfloat16 [64, 128, 5120], P('tm', None, 'tp'), may hold values from -30 to 30
- noise: bfloat16 [64, 128, 5120], P('tm', None, 'tp'), may hold values from -6 to 6
- mod_table: bfloat16 [256, 15360], replicated, may hold values from -0.375 to 0.375
- w_query: bfloat16 [5120, 2560], P('tm', 'tp'), may hold values from -4 to 4
- w_key: bfloat16 [5120, 2560], P('tm', 'tp'), may hold values from -4 to 4
- w_value: bfloat16 [5120, 2560], P('tm', 'tp'), may hold values from -0.078125 to 0.078125
- w_out: bfloat16 [2560, 5120], P('tp', 'tm'), may hold values from -0.125 to 0.125
- step_index: int32 [64], P('tm'), may hold values from 0 to 999
- slide_offset: int32 [], replicated, may hold values from 1 to 2
Outputs:
- window: bfloat16 [64, 128, 5120], P('tm', None, 'tp')
The draws below stay inside these ranges and needn't reach their ends.
All inputs are finite; a program needn't handle non-finite values.
Results may differ from the reference program's by a relative error of at most 0.017.
Values may be sent and summed in bfloat16 or wider, within the bound.
A program may use at most 128 MiB of HBM per device.

```python
import math
import jax
import jax.numpy as jnp
from jax import lax

D = 5120
HEADS = 20
HEAD_SIZE = 128
FREQ = 256
ITERS = 2
STEPS_DEV = 2
LTOK = 128
WINDOW = 64
N_TP = 4


def projection_draw(key):
    entries = jnp.clip(jax.random.normal(key, (D, HEADS * HEAD_SIZE), jnp.float32), -6.0, 6.0) / math.sqrt(D)
    return jnp.clip(entries, -4.0, 4.0).astype(jnp.bfloat16)


def draw_w_query(key, part):
    key = jax.random.fold_in(key, 1)
    return projection_draw(key)


def draw_w_key(key, part):
    key = jax.random.fold_in(key, 2)
    return projection_draw(key)


def draw_latents(key, part):
    key = jax.random.fold_in(key, 3)
    first_key = jax.random.fold_in(key, 0)
    entries = jnp.clip(jax.random.normal(first_key, (WINDOW, LTOK, D), jnp.float32), -6.0, 6.0)
    return jnp.clip(entries, -30.0, 30.0).astype(jnp.bfloat16)


def with_ends(array, own_key, smallest, top_value):
    longest = array.shape.index(max(array.shape))
    spots = []
    for shift in (0, 1):
        where = [jax.random.randint(jax.random.fold_in(own_key, axis), (), 0, length) for axis, length in enumerate(array.shape)]
        where[longest] = (where[longest] + shift) % array.shape[longest]
        spots.append(tuple(where))
    return array.at[spots[0]].set(smallest).at[spots[1]].set(top_value)


def steps_of(rng, dims, cuts, least, largest):
    def one(position, blocks):
        draws = jax.random.uniform(jax.random.fold_in(jax.random.fold_in(rng, 6), position), (blocks,), jnp.float32, least / len(cuts), largest / len(cuts))
        return jnp.repeat(jnp.exp(draws), dims[position] // blocks).reshape((-1,) + (1,) * (len(dims) - position - 1))

    gain = one(*cuts[0])
    for cut in cuts[1:]:
        gain = gain * one(*cut)
    return gain


def bell_draw(key, dims, spread, most, cuts=(), kind=jnp.bfloat16):
    level = steps_of(key, dims, cuts, -0.22, 0.18) if cuts else 1.0
    drawn = jax.random.normal(key, dims, jnp.float32) * spread * level
    return jnp.minimum(jnp.maximum(drawn, -most), most).astype(kind)


def setup_inputs(seed: int = 0) -> dict:
    streams_of = jax.random.split(jax.random.key(seed), 10)
    latents = draw_latents(jax.random.fold_in(streams_of[9], 71), 0)
    noise = bell_draw(streams_of[1], (WINDOW, LTOK, D), 1.0, 6.0, ((0, 32), (2, 4)))
    mod_table = bell_draw(streams_of[2], (FREQ, 3 * D), FREQ ** -0.5, 0.375)
    w_query = draw_w_query(jax.random.fold_in(streams_of[9], 71), 0)
    w_key = draw_w_key(jax.random.fold_in(streams_of[9], 71), 0)
    w_value = bell_draw(streams_of[5], (D, HEADS * HEAD_SIZE), D ** -0.5, 0.078125, ((0, 32), (1, 4)))
    w_out = bell_draw(streams_of[6], (HEADS * HEAD_SIZE, D), (HEADS * HEAD_SIZE) ** -0.5, 0.125, ((0, 4), (1, 32)))
    step_index = with_ends(jax.random.randint(streams_of[7], (WINDOW,), 0, 1000), jax.random.fold_in(streams_of[7], 1), 0, 999).astype(jnp.int32)
    slide_offset = jax.random.randint(streams_of[8], (), 1, STEPS_DEV + 1).astype(jnp.int32)
    return {"latents": latents, "noise": noise, "mod_table": mod_table, "w_query": w_query, "w_key": w_key, "w_value": w_value, "w_out": w_out, "step_index": step_index, "slide_offset": slide_offset}


def rounded_scores(value_rows):
    return lax.optimization_barrier(value_rows.astype(jnp.bfloat16)).astype(jnp.float32)

def modulate(step_index, mod_table):
    half = FREQ // 2
    freqs = jnp.exp(-math.log(10000.0) * jnp.arange(half).astype(jnp.float32) / half)
    angles = step_index.astype(jnp.float32)[:, None] * freqs[None, :]
    feats = jnp.concatenate([jnp.cos(angles), jnp.sin(angles)], axis=1).astype(jnp.bfloat16)
    return jnp.dot(feats, mod_table, preferred_element_type=jnp.float32)

def velocity(latent, modulation, w_query, w_key, w_value, w_out):
    shift = modulation[:D]
    scale = modulation[D:2 * D]
    gate = modulation[2 * D:]
    rows = latent.astype(jnp.float32)
    mean = lax.optimization_barrier(jnp.mean(rows, axis=-1, keepdims=True))
    centred = rows - mean
    var = lax.optimization_barrier(jnp.mean(centred * centred, axis=-1, keepdims=True))
    normed = centred * lax.rsqrt(var + 1e-06)
    inputs = (normed * (1.0 + scale[None, :]) + shift[None, :]).astype(jnp.bfloat16)
    query_rows = rounded_scores(jnp.dot(inputs, w_query, preferred_element_type=jnp.float32)).reshape(LTOK, HEADS, HEAD_SIZE)
    key_rows = rounded_scores(jnp.dot(inputs, w_key, preferred_element_type=jnp.float32)).reshape(LTOK, HEADS, HEAD_SIZE)
    value_rows = rounded_scores(jnp.dot(inputs, w_value, preferred_element_type=jnp.float32)).reshape(LTOK, HEADS, HEAD_SIZE)
    score_matrix = jnp.einsum('vjn,fjn->jvf', query_rows, key_rows) * (1.0 / math.sqrt(HEAD_SIZE))
    top = lax.optimization_barrier(jnp.max(score_matrix, axis=-1, keepdims=True))
    expo = jnp.exp(score_matrix - top)
    attention_probabilities = rounded_scores(expo / lax.optimization_barrier(jnp.sum(expo, axis=-1, keepdims=True)))
    head_outputs = rounded_scores(jnp.einsum('bik,kba->iba', attention_probabilities, value_rows))
    group_width = HEADS * HEAD_SIZE // N_TP
    grouped = head_outputs.reshape(LTOK, N_TP, group_width)
    weights = w_out.astype(jnp.float32).reshape(N_TP, group_width, D)
    partials = rounded_scores(jnp.einsum('lgk,gkd->gld', grouped, weights))
    attn = lax.optimization_barrier(jnp.sum(partials, axis=0))
    return gate[None, :] * attn

def reference(latents, noise, mod_table, w_query, w_key, w_value, w_out, step_index, slide_offset):
    modulation = modulate(step_index, mod_table)
    step_size = (step_index.astype(jnp.float32) + 1.0) / 2000.0
    noise_size = 0.2 * jnp.sqrt(step_size)
    first = latents[0].astype(jnp.float32)
    current = latents
    for iteration in range(ITERS):
        drift = lax.map(lambda pair: velocity(pair[0], pair[1], w_query, w_key, w_value, w_out), (current, modulation))
        terms = step_size[:, None, None] * drift + noise_size[:, None, None] * noise.astype(jnp.float32)
        running = jnp.cumsum(terms, axis=0)
        current = jnp.concatenate([first[None], first[None] + running[:-1]], axis=0).astype(jnp.bfloat16)
    positions = jnp.minimum(jnp.arange(WINDOW).astype(jnp.int32) + slide_offset.astype(jnp.int32), WINDOW - 1)
    return current[positions]
```

```python
import functools
import math

import jax
import jax.numpy as jnp
from jax import lax
from jax.experimental import pallas as pl
from jax.experimental.pallas import tpu as pltpu
from jax.sharding import PartitionSpec as P

HEAD_SIZE = 128
HEADS = 5
ITERS = 2
TOK = 128
ROWS = 256
QUART = 1280
WIDTH = 5120
HW = 640
SHARD = 160
HALF = 80
MESH = pl.DeviceIdType.MESH
F32 = jnp.float32
BF16 = jnp.bfloat16
N_MSG = 36


def kernel(
    lat_ref, noise_ref, table_ref, wq_ref, wk_ref, wv_ref, wo_ref, feats_ref, hg_ref, off_ref,
    out_ref,
    w, cur, y, acc, qkv, heads, part, rs_d2, rs_fin, t, x0, nz, mods, stat,
    tf, px_s, px_r, p1_s, p1_r, p2_s, p2_r, pe_s, pe_r, pfx, sl_s, sl_r,
    loc_sem, w_ss, w_rs, ag_ss, ag_rs, rs_ss, rs_rs, px_ss, px_rs,
):
    tm = lax.axis_index("tm")
    x = lax.axis_index("tp")
    core = lax.rem(tm, 2)
    chip = lax.div(tm, 2)
    yy, zz = lax.div(chip, 4), lax.rem(chip, 4)
    is0 = core == 0
    a = jnp.where(is0, zz, yy)
    b = jnp.where(is0, yy, zz)

    def rank(da, db):
        aa, bb = lax.rem(a + da, 4), lax.rem(b + db, 4)
        return jnp.where(is0, bb * 4 + aa, aa * 4 + bb) * 2 + core

    def dev(da, db):
        return (rank(da, db), x)

    sib = (tm + 1 - 2 * core, x)
    xp = (tm, lax.rem(x + 1, 4))
    xm = (tm, lax.rem(x + 3, 4))
    following = (lax.rem(tm + 1, 32), x)
    before = (lax.rem(tm + 31, 32), x)
    x1, x2, x3 = lax.rem(x + 1, 4), lax.rem(x + 2, 4), lax.rem(x + 3, 4)

    def remote(src, dst, ss, rs, to):
        return pltpu.make_async_remote_copy(
            src_ref=src, dst_ref=dst, send_sem=ss, recv_sem=rs, device_id=to, device_id_type=MESH
        )

    own = pl.ds(pl.multiple_of(SHARD * tm, 16), SHARD)
    local = [
        pltpu.make_async_copy(src, w.at[k, own], loc_sem.at[k])
        for k, src in enumerate((wq_ref, wk_ref, wv_ref, wo_ref))
    ]
    local.append(pltpu.make_async_copy(lat_ref, cur.at[0, x], loc_sem.at[4]))
    local.append(pltpu.make_async_copy(noise_ref, nz, loc_sem.at[5]))
    for c in local:
        c.start()

    barrier = pltpu.get_barrier_semaphore()
    peers = [sib, xp, xm, following, before]
    peers += [dev(k, 0) for k in (1, 2, 3)] + [dev(0, k) for k in (1, 2, 3)]
    for peer in peers:
        pl.semaphore_signal(barrier, inc=1, device_id=peer, device_id_type=MESH)
    pl.semaphore_wait(barrier, len(peers))

    for c in local:
        c.wait()

    def ag_msg(it, m):
        to = xp if m in (0, 2, 4) else xm
        src = (x, x, x, x, x3, x1)[m]
        step = (0, 1, 1, 0, 0, 1)[m]
        ref = cur.at[it, src, pl.ds(TOK * step, TOK)]
        return remote(ref, ref, ag_ss.at[it, m], ag_rs.at[it, m], to)

    def ag_start(it):
        for m in range(4):
            ag_msg(it, m).start()

    def ag_forward(it):
        ag_msg(it, 0).wait_recv()
        ag_msg(it, 4).start()
        ag_msg(it, 1).wait_recv()
        ag_msg(it, 5).start()

    def ag_finish(it):
        for m in (2, 3, 4, 5):
            ag_msg(it, m).wait_recv()
        for m in range(6):
            ag_msg(it, m).wait_send()

    def rows_of(r, lo, n):
        return pl.ds(pl.multiple_of(SHARD * r + lo, 16), n)

    def w_msg(k, m):
        if m < 4:
            ref = (
                w.at[k, rows_of(tm, 0, SHARD)],
                w.at[k, rows_of(tm, 0, SHARD)],
                w.at[k, rows_of(rank(3, 0), 0, HALF)],
                w.at[k, rows_of(rank(1, 0), HALF, HALF)],
            )[m]
            to = dev(1, 0) if m in (0, 2) else dev(3, 0)
        elif m < 20:
            j, i = divmod(m - 4, 4)
            da = (0, 3, 1, 2)[j]
            ref = (
                w.at[k, rows_of(rank(da, 0), 0, SHARD)],
                w.at[k, rows_of(rank(da, 0), 0, SHARD)],
                w.at[k, rows_of(rank(da, 3), 0, HALF)],
                w.at[k, rows_of(rank(da, 1), HALF, HALF)],
            )[i]
            to = dev(0, 1) if i in (0, 2) else dev(0, 3)
        else:
            j, i = divmod(m - 20, 4)
            ref = w.at[k, rows_of(rank((0, 3, 1, 2)[j], (0, 3, 1, 2)[i]), 0, SHARD)]
            to = sib
        return remote(ref, ref, w_ss.at[k, m], w_rs.at[k, m], to)

    def w_start(k, *ms):
        for m in ms:
            w_msg(k, m).start()

    def w_recv(k, *ms):
        for m in ms:
            w_msg(k, m).wait_recv()

    def s0(k):
        w_start(k, 0, 1, 4, 5, 20)

    def s1(k):
        w_recv(k, 0)
        w_start(k, 2, 8, 9, 24)
        w_recv(k, 1)
        w_start(k, 3, 12, 13, 28)

    def s2(k):
        w_recv(k, 2, 3)
        w_start(k, 16, 17, 32)

    def s3(k):
        for j in range(4):
            w_recv(k, 4 + 4 * j)
            w_start(k, 6 + 4 * j, 21 + 4 * j)
            w_recv(k, 5 + 4 * j)
            w_start(k, 7 + 4 * j, 22 + 4 * j)

    def s5(k):
        for j in range(4):
            w_recv(k, 6 + 4 * j, 7 + 4 * j)
            w_start(k, 23 + 4 * j)

    def s6(k):
        for m in range(20, 36):
            w_msg(k, m).wait_recv()

    def w_sent(k):
        for m in range(N_MSG):
            w_msg(k, m).wait_send()

    def modulation():
        for base in (0, 4, 8):
            count = 4 if base < 8 else 1
            for k in range(count):
                start = (base + k) * QUART if base < 8 else 2 * WIDTH + x * QUART
                pltpu.make_async_copy(
                    table_ref.at[:, pl.ds(pl.multiple_of(start, 128), QUART)],
                    part.at[k], loc_sem.at[k],
                ).start()
            for k in range(count):
                pltpu.make_async_copy(
                    table_ref.at[:, pl.ds(0, QUART)], part.at[k], loc_sem.at[k]
                ).wait()
                mods[base + k] = jnp.dot(feats_ref[...], part[k], preferred_element_type=F32)

    def norm(it):
        def body(i, carry):
            rows = pl.ds(pl.multiple_of(16 * i, 16), 16)
            step = lax.div(i, 8)
            total = jnp.zeros((16, 1), F32)
            for q in range(4):
                total += jnp.sum(cur[it, q, rows].astype(F32), axis=-1, keepdims=True)
            mean = total / WIDTH
            square = jnp.zeros((16, 1), F32)
            for q in range(4):
                d = cur[it, q, rows].astype(F32) - mean
                square += jnp.sum(d * d, axis=-1, keepdims=True)
            inv = lax.rsqrt(square / WIDTH + 1e-6)
            for q in range(4):
                d = (cur[it, q, rows].astype(F32) - mean) * inv
                shift = mods[q, pl.ds(step, 1)]
                scale = mods[4 + q, pl.ds(step, 1)]
                y[q, rows] = (d * (1.0 + scale) + shift).astype(BF16)
            return carry

        lax.fori_loop(0, 16, body, 0)

    def project(k):
        def body(q, carry):
            rows = pl.ds(pl.multiple_of(q * QUART, 128), QUART)
            acc[...] += jnp.dot(y[q], w[k, rows], preferred_element_type=F32)
            return carry

        acc[...] = jnp.zeros_like(acc)
        lax.fori_loop(0, 4, body, 0)
        qkv[k] = acc[...].astype(BF16)

    def attention():
        for step in range(2):
            for h in range(HEADS):
                rows, cols = pl.ds(TOK * step, TOK), pl.ds(HEAD_SIZE * h, HEAD_SIZE)
                s = lax.dot_general(
                    qkv[0, rows, cols], qkv[1, rows, cols], (((1,), (1,)), ((), ())),
                    preferred_element_type=F32,
                ) * (1.0 / math.sqrt(HEAD_SIZE))
                e = jnp.exp(s - jnp.max(s, axis=-1, keepdims=True))
                p = (e / jnp.sum(e, axis=-1, keepdims=True)).astype(BF16)
                heads[rows, cols] = jnp.dot(
                    p, qkv[2, rows, cols], preferred_element_type=F32
                ).astype(BF16)

    def out_part(q):
        def body(i, carry):
            rows = pl.ds(pl.multiple_of(q * QUART + i * 256, 128), 256)
            cols = pl.ds(pl.multiple_of(i * 256, 128), 256)
            part[q, :, cols] = lax.dot_general(
                heads[...], w[3, rows], (((1,), (1,)), ((), ())), preferred_element_type=F32
            ).astype(BF16)
            return carry

        lax.fori_loop(0, 5, body, 0)

    def rs_msg(it, m):
        step = (0, 1, 1, 0, 0, 1)[m]
        to = xp if m in (0, 2, 4) else xm
        rows = pl.ds(TOK * step, TOK)
        if m < 2:
            src, dst = part.at[x2, rows], rs_d2.at[it, m]
        elif m in (2, 4):
            src, dst = part.at[x1, rows], rs_fin.at[it, 0, rows]
        else:
            src, dst = part.at[x3, rows], rs_fin.at[it, 1, rows]
        return remote(src, dst, rs_ss.at[it, m], rs_rs.at[it, m], to)

    def add_in(it, m, q):
        step = (0, 1)[m]

        def body(i, carry):
            rows = pl.ds(pl.multiple_of(TOK * step + 16 * i, 16), 16)
            there = pl.ds(pl.multiple_of(16 * i, 16), 16)
            part[q, rows] = (part[q, rows].astype(F32) + rs_d2[it, m, there].astype(F32)).astype(BF16)
            return carry

        lax.fori_loop(0, 8, body, 0)

    def reduce_out(it):
        out_part(x2)
        rs_msg(it, 0).start()
        rs_msg(it, 1).start()
        out_part(x1)
        rs_msg(it, 2).start()
        out_part(x3)
        rs_msg(it, 3).start()
        rs_msg(it, 0).wait_recv()
        add_in(it, 0, x1)
        rs_msg(it, 4).start()
        rs_msg(it, 1).wait_recv()
        add_in(it, 1, x3)
        rs_msg(it, 5).start()
        out_part(x)
        for m in (2, 3, 4, 5):
            rs_msg(it, m).wait_recv()
        for m in range(6):
            rs_msg(it, m).wait_send()

    first = jnp.where(tm == 0, 1.0, 0.0).astype(F32)

    def terms(it):
        def body(i, carry):
            rows = pl.ds(pl.multiple_of(16 * i, 16), 16)
            step = lax.div(i, 8)
            attn = (
                part[x, rows].astype(F32)
                + rs_fin[it, 0, rows].astype(F32)
                + rs_fin[it, 1, rows].astype(F32)
            )
            gate = mods[8, pl.ds(step, 1)] * hg_ref[step]
            t[rows] = gate * attn + hg_ref[2 + step] * nz[rows].astype(F32)
            return carry

        lax.fori_loop(0, 16, body, 0)

        def body2(i, carry):
            rows = pl.ds(pl.multiple_of(16 * i, 16), 16)
            rows1 = pl.ds(pl.multiple_of(TOK + 16 * i, 16), 16)
            tf[rows] = t[rows] + t[rows1] + first * cur[0, x, rows].astype(F32)
            return carry

        lax.fori_loop(0, 8, body2, 0)

    mine = pl.ds(pl.multiple_of(64 * core, 64), 64)
    other = pl.ds(pl.multiple_of(64 - 64 * core, 64), 64)
    on0 = jnp.where(is0, 1.0, 0.0).astype(F32)
    on1 = 1.0 - on0

    def px_msg(it, m):
        if m == 0:
            src, dst, to = px_s, px_r.at[it], sib
        elif m < 4:
            src, dst, to = p1_s, p1_r.at[it, m - 1], dev(m, 0)
        elif m < 7:
            src, dst, to = p2_s.at[m - 4], p2_r.at[it, m - 4], dev(0, m - 3)
        elif m == 7:
            src, dst, to = pe_s, pe_r.at[it], sib
        else:
            src, dst, to = sl_s, sl_r, before
        return remote(src, dst, px_ss.at[it, m], px_rs.at[it, m], to)

    def prefix(it):
        px_s[...] = tf[other].astype(BF16)
        px_msg(it, 0).start()
        if it == ITERS - 1:
            sl_s[...] = t[0:TOK].astype(BF16)
            px_msg(it, 8).start()
        px_msg(it, 0).wait_recv()

        def loop(f):
            def body(i, carry):
                f(pl.ds(pl.multiple_of(16 * i, 16), 16),
                  pl.ds(pl.multiple_of(64 * core + 16 * i, 16), 16))
                return carry

            lax.fori_loop(0, 4, body, 0)

        def one(r, m):
            p1_s[r] = (tf[m] + px_r[it, r].astype(F32)).astype(BF16)

        loop(one)
        for k in (1, 3, 2):
            px_msg(it, k).start()
        for k in (1, 3, 2):
            px_msg(it, k).wait_recv()

        def two(r, m):
            chip_sum = tf[m] + px_r[it, r].astype(F32)
            lower = jnp.zeros((16, QUART), F32)
            total = chip_sum
            for k in (1, 2, 3):
                there = p1_r[it, k - 1, r].astype(F32)
                total += there
                lower += jnp.where(k <= a, 1.0, 0.0).astype(F32) * there
            pfx[m] = lower
            for k in (1, 2, 3):
                up = jnp.where(b + k < 4, 1.0, 0.0).astype(F32)
                p2_s[k - 1, r] = (on0 * total + on1 * (lower + up * chip_sum)).astype(BF16)

        loop(two)
        for k in (4, 6, 5):
            px_msg(it, k).start()
        for k in (4, 6, 5):
            px_msg(it, k).wait_recv()

        def three(r, m):
            p = pfx[m]
            for k in (1, 2, 3):
                keep = jnp.where(is0 & (k > b), 0.0, 1.0).astype(F32)
                p += keep * p2_r[it, k - 1, r].astype(F32)
            pe_s[r] = (p + on0 * tf[m]).astype(BF16)
            pfx[m] = p + on1 * px_r[it, r].astype(F32)

        loop(three)
        px_msg(it, 7).start()
        px_msg(it, 7).wait_recv()
        pfx[other] = pe_r[it].astype(F32)
        for m in range(8 + (it == ITERS - 1)):
            px_msg(it, m).wait_send()

    def advance(it):
        def body(i, carry):
            rows = pl.ds(pl.multiple_of(16 * i, 16), 16)
            rows1 = pl.ds(pl.multiple_of(TOK + 16 * i, 16), 16)
            p = pfx[rows] + first * cur[0, x, rows].astype(F32)
            cur[it + 1, x, rows] = p.astype(BF16)
            cur[it + 1, x, rows1] = (p + t[rows]).astype(BF16)
            return carry

        lax.fori_loop(0, 8, body, 0)

    def slide():
        px_msg(ITERS - 1, 8).wait_recv()
        one = off_ref[0] == 1
        last = tm == 31

        def body(i, carry):
            rows = pl.ds(pl.multiple_of(16 * i, 16), 16)
            rows1 = pl.ds(pl.multiple_of(TOK + 16 * i, 16), 16)
            c1 = pfx[rows] + first * cur[0, x, rows].astype(F32) + t[rows]
            c2 = c1 + t[rows1]
            c3 = c2 + sl_r[rows].astype(F32)
            c2 = jnp.where(last, c1, c2)
            c3 = jnp.where(last, c1, c3)
            out_ref[rows] = jnp.where(one, c1, c2).astype(BF16)
            out_ref[rows1] = jnp.where(one, c2, c3).astype(BF16)
            return carry

        lax.fori_loop(0, 8, body, 0)

    ag_start(0)
    for k in range(4):
        s0(k)
    s1(0)
    s2(0)
    ag_forward(0)
    modulation()
    s1(1)
    s2(1)
    ag_finish(0)
    norm(0)

    def weights(k, carry):
        s3(k)

        @pl.when(k < 2)
        def _():
            s1(k + 2)
            s2(k + 2)

        s5(k)
        s6(k)
        project(k)
        return carry

    lax.fori_loop(0, 3, weights, 0)
    attention()
    s3(3)
    s5(3)
    s6(3)
    reduce_out(0)
    terms(0)
    prefix(0)
    advance(0)
    lax.fori_loop(0, 4, lambda k, c: (w_sent(k), c)[1], 0)

    ag_start(1)
    ag_forward(1)
    ag_finish(1)
    norm(1)
    lax.fori_loop(0, 3, lambda k, c: (project(k), c)[1], 0)
    attention()
    reduce_out(1)
    terms(1)
    prefix(1)
    slide()


def features(step_index, mod_table):
    half = mod_table.shape[0] // 2
    freqs = jnp.exp(-math.log(10000.0) * jnp.arange(half).astype(F32) / half)
    angles = step_index.astype(F32)[:, None] * freqs[None, :]
    return jnp.concatenate([jnp.cos(angles), jnp.sin(angles)], axis=1).astype(BF16)


def per_device(latents, noise, mod_table, w_query, w_key, w_value, w_out, step_index, slide_offset):
    feats = features(step_index, mod_table)
    feats = jnp.concatenate([feats, jnp.zeros((14, feats.shape[1]), BF16)], axis=0)
    step_size = (step_index.astype(F32) + 1.0) / 2000.0
    hg = jnp.concatenate([step_size, 0.2 * jnp.sqrt(step_size)])
    hbm = pl.BlockSpec(memory_space=pl.ANY)
    vmem = pl.BlockSpec(memory_space=pltpu.VMEM)
    smem = pl.BlockSpec(memory_space=pltpu.SMEM)
    dma = pltpu.SemaphoreType.DMA
    out = pl.pallas_call(
        kernel,
        out_shape=jax.ShapeDtypeStruct((ROWS, QUART), BF16),
        in_specs=[hbm] * 7 + [vmem, smem, smem],
        out_specs=vmem,
        scratch_shapes=[
            pltpu.VMEM((4, WIDTH, HW), BF16),
            pltpu.VMEM((ITERS, 4, ROWS, QUART), BF16),
            pltpu.VMEM((4, ROWS, QUART), BF16),
            pltpu.VMEM((ROWS, HW), F32),
            pltpu.VMEM((3, ROWS, HW), BF16),
            pltpu.VMEM((ROWS, HW), BF16),
            pltpu.VMEM((4, ROWS, QUART), BF16),
            pltpu.VMEM((ITERS, 2, TOK, QUART), BF16),
            pltpu.VMEM((ITERS, 2, ROWS, QUART), BF16),
            pltpu.VMEM((ROWS, QUART), F32),
            pltpu.VMEM((16, 128), BF16),
            pltpu.VMEM((ROWS, QUART), BF16),
            pltpu.VMEM((9, 16, QUART), F32),
            pltpu.VMEM((8, 128), F32),
            pltpu.VMEM((TOK, QUART), F32),
            pltpu.VMEM((64, QUART), BF16),
            pltpu.VMEM((ITERS, 64, QUART), BF16),
            pltpu.VMEM((64, QUART), BF16),
            pltpu.VMEM((ITERS, 3, 64, QUART), BF16),
            pltpu.VMEM((3, 64, QUART), BF16),
            pltpu.VMEM((ITERS, 3, 64, QUART), BF16),
            pltpu.VMEM((64, QUART), BF16),
            pltpu.VMEM((ITERS, 64, QUART), BF16),
            pltpu.VMEM((TOK, QUART), F32),
            pltpu.VMEM((TOK, QUART), BF16),
            pltpu.VMEM((TOK, QUART), BF16),
            dma((6,)),
            dma((4, N_MSG)),
            dma((4, N_MSG)),
            dma((ITERS, 6)),
            dma((ITERS, 6)),
            dma((ITERS, 6)),
            dma((ITERS, 6)),
            dma((ITERS, 9)),
            dma((ITERS, 9)),
        ],
        compiler_params=pltpu.CompilerParams(
            collective_id=0, has_side_effects=True, vmem_limit_bytes=62 * 1024 * 1024
        ),
        cost_estimate=pl.CostEstimate(
            flops=2 * ITERS * 4 * ROWS * WIDTH * HW, bytes_accessed=12_000_000, transcendentals=0
        ),
    )(
        latents.reshape(ROWS, QUART), noise.reshape(ROWS, QUART), mod_table,
        w_query, w_key, w_value, w_out.T, feats, hg, slide_offset.reshape(1),
    )
    return out.reshape(latents.shape)


def solution(mesh):
    placed = (
        P("tm", None, "tp"),
        P("tm", None, "tp"),
        P(),
        P("tm", "tp"),
        P("tm", "tp"),
        P("tm", "tp"),
        P("tp", "tm"),
        P("tm"),
        P(),
    )
    return jax.shard_map(
        per_device, mesh=mesh, in_specs=placed, out_specs=P("tm", None, "tp"), check_vma=False
    )
```

```python
import functools
import math

import jax
import jax.numpy as jnp
from jax import lax
from jax.experimental import pallas as pl
from jax.experimental.pallas import tpu as pltpu
from jax.sharding import PartitionSpec as P

HEAD_SIZE = 128
HEADS = 5
ITERS = 2
TOK = 128
ROWS = 256
QUART = 1280
WIDTH = 5120
HW = 640
SHARD = 160
HALF = 80
MESH = pl.DeviceIdType.MESH
F32 = jnp.float32
BF16 = jnp.bfloat16
N_MSG = 36


def kernel(
    lat_ref, noise_ref, table_ref, wq_ref, wk_ref, wv_ref, wo_ref, feats_ref, hg_ref, off_ref,
    out_ref,
    w, cur, y, acc, qkv, hd, part, tb, t, nz, mods, stat,
    tf, px_s, px_r, p1_s, p1_r, p2_s, p2_r, pe_s, pe_r, pfx, sl_s, sl_r,
    loc_sem, w_ss, w_rs, ag_ss, ag_rs, hd_ss, hd_rs, px_ss, px_rs, tr_ss, tr_rs,
):
    tm = lax.axis_index("tm")
    x = lax.axis_index("tp")
    core = lax.rem(tm, 2)
    chip = lax.div(tm, 2)
    yy, zz = lax.div(chip, 4), lax.rem(chip, 4)
    is0 = core == 0
    a = jnp.where(is0, zz, yy)
    b = jnp.where(is0, yy, zz)

    def rank(da, db):
        aa, bb = lax.rem(a + da, 4), lax.rem(b + db, 4)
        return jnp.where(is0, bb * 4 + aa, aa * 4 + bb) * 2 + core

    def dev(da, db):
        return (rank(da, db), x)

    sib = (tm + 1 - 2 * core, x)
    xp = (tm, lax.rem(x + 1, 4))
    xm = (tm, lax.rem(x + 3, 4))
    following = (lax.rem(tm + 1, 32), x)
    before = (lax.rem(tm + 31, 32), x)
    swapped = ((x * 4 + zz) * 2 + core, yy)
    swaps = x != yy
    x1, x2, x3 = lax.rem(x + 1, 4), lax.rem(x + 2, 4), lax.rem(x + 3, 4)

    def remote(src, dst, ss, rs, to):
        return pltpu.make_async_remote_copy(
            src_ref=src, dst_ref=dst, send_sem=ss, recv_sem=rs, device_id=to, device_id_type=MESH
        )

    own = pl.ds(pl.multiple_of(SHARD * tm, 16), SHARD)
    local = [
        pltpu.make_async_copy(src, w.at[k, own], loc_sem.at[k])
        for k, src in enumerate((wq_ref, wk_ref, wv_ref))
    ]
    local.append(pltpu.make_async_copy(lat_ref, cur.at[0, x], loc_sem.at[4]))
    local.append(pltpu.make_async_copy(noise_ref, nz, loc_sem.at[5]))
    for c in local:
        c.start()

    barrier = pltpu.get_barrier_semaphore()
    peers = [sib, xp, xm, following, before]
    peers += [dev(k, 0) for k in (1, 2, 3)] + [dev(0, k) for k in (1, 2, 3)]
    for peer in peers:
        pl.semaphore_signal(barrier, inc=1, device_id=peer, device_id_type=MESH)

    @pl.when(swaps)
    def _():
        pl.semaphore_signal(barrier, inc=1, device_id=swapped, device_id_type=MESH)

    pl.semaphore_wait(barrier, len(peers) + jnp.where(swaps, 1, 0))

    def swap_msg():
        there = pl.ds(pl.multiple_of(SHARD * swapped[0], 16), SHARD)
        return remote(wo_ref, w.at[3, there], tr_ss, tr_rs, swapped)

    def swap_local():
        return pltpu.make_async_copy(wo_ref, w.at[3, own], loc_sem.at[3])

    @pl.when(swaps)
    def _():
        swap_msg().start()

    @pl.when(jnp.logical_not(swaps))
    def _():
        swap_local().start()

    def swap_finish():
        @pl.when(swaps)
        def _():
            swap_msg().wait()

        @pl.when(jnp.logical_not(swaps))
        def _():
            swap_local().wait()

    for c in local:
        c.wait()

    class Gather:
        def __init__(self, block, halves, ss, rs):
            self.block, self.halves, self.ss, self.rs = block, halves, ss, rs

        def msg(self, m):
            to = xp if m in (0, 2, 4) else xm
            src = (x, x, x, x, x3, x1)[m]
            ref = self.block(src, self.halves[(0, 1, 1, 0, 0, 1)[m]])
            return remote(ref, ref, self.ss(m), self.rs(m), to)

        def start(self, *ms):
            for m in ms:
                self.msg(m).start()

        def forward(self):
            self.msg(0).wait_recv()
            self.msg(4).start()
            self.msg(1).wait_recv()
            self.msg(5).start()

        def recv(self, *ms):
            for m in ms:
                self.msg(m).wait_recv()

        def sent(self):
            for m in range(6):
                self.msg(m).wait_send()

    steps = (pl.ds(0, TOK), pl.ds(TOK, TOK))
    lat_g = Gather(lambda q, r: cur.at[0, q, r], steps, lambda m: ag_ss.at[0, m], lambda m: ag_rs.at[0, m])
    t0_g = Gather(
        lambda q, r: tb.at[q, r], (pl.ds(0, 64), pl.ds(64, 64)),
        lambda m: ag_ss.at[1, m], lambda m: ag_rs.at[1, m],
    )
    pfx_g = Gather(
        lambda q, r: cur.at[1, q, r],
        (pl.ds(pl.multiple_of(64 * core, 64), 64), pl.ds(pl.multiple_of(64 - 64 * core, 64), 64)),
        lambda m: ag_ss.at[2, m], lambda m: ag_rs.at[2, m],
    )
    hd_g = [
        Gather(
            lambda q, r, it=it: hd.at[it, q, r], steps,
            lambda m, it=it: hd_ss.at[it, m], lambda m, it=it: hd_rs.at[it, m],
        )
        for it in range(ITERS)
    ]

    def rows_of(r, lo, n):
        return pl.ds(pl.multiple_of(SHARD * r + lo, 16), n)

    def w_msg(k, m):
        if m < 4:
            ref = (
                w.at[k, rows_of(tm, 0, SHARD)],
                w.at[k, rows_of(tm, 0, SHARD)],
                w.at[k, rows_of(rank(3, 0), 0, HALF)],
                w.at[k, rows_of(rank(1, 0), HALF, HALF)],
            )[m]
            to = dev(1, 0) if m in (0, 2) else dev(3, 0)
        elif m < 20:
            j, i = divmod(m - 4, 4)
            da = (0, 3, 1, 2)[j]
            ref = (
                w.at[k, rows_of(rank(da, 0), 0, SHARD)],
                w.at[k, rows_of(rank(da, 0), 0, SHARD)],
                w.at[k, rows_of(rank(da, 3), 0, HALF)],
                w.at[k, rows_of(rank(da, 1), HALF, HALF)],
            )[i]
            to = dev(0, 1) if i in (0, 2) else dev(0, 3)
        else:
            j, i = divmod(m - 20, 4)
            ref = w.at[k, rows_of(rank((0, 3, 1, 2)[j], (0, 3, 1, 2)[i]), 0, SHARD)]
            to = sib
        return remote(ref, ref, w_ss.at[k, m], w_rs.at[k, m], to)

    def w_start(k, *ms):
        for m in ms:
            w_msg(k, m).start()

    def w_recv(k, *ms):
        for m in ms:
            w_msg(k, m).wait_recv()

    def s0(k):
        w_start(k, 0, 1, 4, 5, 20)

    def s1(k):
        w_recv(k, 0)
        w_start(k, 2, 8, 9, 24)
        w_recv(k, 1)
        w_start(k, 3, 12, 13, 28)

    def s2(k):
        w_recv(k, 2, 3)
        w_start(k, 16, 17, 32)

    def s3(k):
        for j in range(4):
            w_recv(k, 4 + 4 * j)
            w_start(k, 6 + 4 * j, 21 + 4 * j)
            w_recv(k, 5 + 4 * j)
            w_start(k, 7 + 4 * j, 22 + 4 * j)

    def s5(k):
        for j in range(4):
            w_recv(k, 6 + 4 * j, 7 + 4 * j)
            w_start(k, 23 + 4 * j)

    def s6(k):
        for m in range(20, 36):
            w_msg(k, m).wait_recv()

    def w_sent(k):
        for m in range(N_MSG):
            w_msg(k, m).wait_send()

    def modulation():
        for base in (0, 4, 8):
            count = 4 if base < 8 else 1
            for k in range(count):
                start = (base + k) * QUART if base < 8 else 2 * WIDTH + x * QUART
                pltpu.make_async_copy(
                    table_ref.at[:, pl.ds(pl.multiple_of(start, 128), QUART)],
                    part.at[k], loc_sem.at[k],
                ).start()
            for k in range(count):
                pltpu.make_async_copy(
                    table_ref.at[:, pl.ds(0, QUART)], part.at[k], loc_sem.at[k]
                ).wait()
                mods[base + k] = jnp.dot(feats_ref[...], part[k], preferred_element_type=F32)

    def block_stats(it, q):
        def body(i, carry):
            rows = pl.ds(pl.multiple_of(16 * i, 16), 16)
            c = cur[it, q, rows].astype(F32)
            mean = jnp.sum(c, axis=-1, keepdims=True) / QUART
            d = c - mean
            stat[q, 0, rows] = jnp.broadcast_to(mean, (16, 128))
            stat[q, 1, rows] = jnp.broadcast_to(jnp.sum(d * d, axis=-1, keepdims=True), (16, 128))
            return carry

        lax.fori_loop(0, 16, body, 0)

    def block_second(q):
        def body(i, carry):
            rows = pl.ds(pl.multiple_of(16 * i, 16), 16)
            rows1 = pl.ds(pl.multiple_of(TOK + 16 * i, 16), 16)
            cur[1, q, rows1] = (cur[1, q, rows].astype(F32) + tb[q, rows].astype(F32)).astype(BF16)
            return carry

        lax.fori_loop(0, 8, body, 0)

    def norm(it):
        def body(i, carry):
            rows = pl.ds(pl.multiple_of(16 * i, 16), 16)
            step = lax.div(i, 8)
            means = [stat[q, 0, rows][:, :1] for q in range(4)]
            mean = (means[0] + means[1] + means[2] + means[3]) * 0.25
            square = jnp.zeros((16, 1), F32)
            for q in range(4):
                off = means[q] - mean
                square += stat[q, 1, rows][:, :1] + QUART * off * off
            inv = lax.rsqrt(square / WIDTH + 1e-6)
            for q in range(4):
                d = (cur[it, q, rows].astype(F32) - mean) * inv
                shift = mods[q, pl.ds(step, 1)]
                scale = mods[4 + q, pl.ds(step, 1)]
                y[q, rows] = (d * (1.0 + scale) + shift).astype(BF16)
            return carry

        lax.fori_loop(0, 16, body, 0)

    def project(k):
        def body(q, carry):
            rows = pl.ds(pl.multiple_of(q * QUART, 128), QUART)
            acc[...] += jnp.dot(y[q], w[k, rows], preferred_element_type=F32)
            return carry

        acc[...] = jnp.zeros_like(acc)
        lax.fori_loop(0, 4, body, 0)
        qkv[k] = acc[...].astype(BF16)

    def attention(it):
        for step in range(2):
            for h in range(HEADS):
                rows, cols = pl.ds(TOK * step, TOK), pl.ds(HEAD_SIZE * h, HEAD_SIZE)
                s = lax.dot_general(
                    qkv[0, rows, cols], qkv[1, rows, cols], (((1,), (1,)), ((), ())),
                    preferred_element_type=F32,
                ) * (1.0 / math.sqrt(HEAD_SIZE))
                e = jnp.exp(s - jnp.max(s, axis=-1, keepdims=True))
                p = (e / jnp.sum(e, axis=-1, keepdims=True)).astype(BF16)
                hd[it, x, rows, cols] = jnp.dot(
                    p, qkv[2, rows, cols], preferred_element_type=F32
                ).astype(BF16)
            if step == 0:
                hd_g[it].start(0, 3)
            else:
                hd_g[it].start(1, 2)

    def out_part(it, q, add):
        def body(i, carry):
            rows = pl.ds(pl.multiple_of(q * QUART + i * 256, 128), 256)
            cols = pl.ds(pl.multiple_of(i * 256, 128), 256)
            new = lax.dot_general(
                hd[it, q], w[3, rows], (((1,), (1,)), ((), ())), preferred_element_type=F32
            )
            t[:, cols] = t[:, cols] + new if add else new
            return carry

        lax.fori_loop(0, 5, body, 0)

    def out_project(it):
        g = hd_g[it]
        out_part(it, x, False)
        g.recv(2)
        out_part(it, x3, True)
        g.recv(3)
        out_part(it, x1, True)
        g.recv(4, 5)
        out_part(it, x2, True)

    first = jnp.where(tm == 0, 1.0, 0.0).astype(F32)

    def terms(it):
        def body(i, carry):
            rows = pl.ds(pl.multiple_of(16 * i, 16), 16)
            step = lax.div(i, 8)
            gate = mods[8, pl.ds(step, 1)] * hg_ref[step]
            t[rows] = gate * t[rows] + hg_ref[2 + step] * nz[rows].astype(F32)
            return carry

        lax.fori_loop(0, 16, body, 0)

        def body2(i, carry):
            rows = pl.ds(pl.multiple_of(16 * i, 16), 16)
            rows1 = pl.ds(pl.multiple_of(TOK + 16 * i, 16), 16)
            t0 = t[rows]
            tf[rows] = t0 + t[rows1] + first * cur[0, x, rows].astype(F32)
            if it == 0:
                tb[x, rows] = t0.astype(BF16)
            return carry

        lax.fori_loop(0, 8, body2, 0)

    mine = pl.ds(pl.multiple_of(64 * core, 64), 64)
    other = pl.ds(pl.multiple_of(64 - 64 * core, 64), 64)
    on0 = jnp.where(is0, 1.0, 0.0).astype(F32)
    on1 = 1.0 - on0

    def px_msg(it, m):
        if m == 0:
            src, dst, to = px_s, px_r.at[it], sib
        elif m < 4:
            src, dst, to = p1_s, p1_r.at[it, m - 1], dev(m, 0)
        elif m < 7:
            src, dst, to = p2_s.at[m - 4], p2_r.at[it, m - 4], dev(0, m - 3)
        elif m == 7:
            src, dst, to = pe_s, pe_r.at[it], sib
        else:
            src, dst, to = sl_s, sl_r, before
        return remote(src, dst, px_ss.at[it, m], px_rs.at[it, m], to)

    def prefix(it):
        px_s[...] = tf[other].astype(BF16)
        px_msg(it, 0).start()
        if it == ITERS - 1:
            sl_s[...] = t[0:TOK].astype(BF16)
            px_msg(it, 8).start()
        px_msg(it, 0).wait_recv()

        def loop(f):
            def body(i, carry):
                f(pl.ds(pl.multiple_of(16 * i, 16), 16),
                  pl.ds(pl.multiple_of(64 * core + 16 * i, 16), 16))
                return carry

            lax.fori_loop(0, 4, body, 0)

        def one(r, m):
            p1_s[r] = (tf[m] + px_r[it, r].astype(F32)).astype(BF16)

        loop(one)
        for k in (1, 3, 2):
            px_msg(it, k).start()
        for k in (1, 3, 2):
            px_msg(it, k).wait_recv()
        if it == 0:
            t0_g.forward()

        def two(r, m):
            chip_sum = tf[m] + px_r[it, r].astype(F32)
            lower = jnp.zeros((16, QUART), F32)
            total = chip_sum
            for k in (1, 2, 3):
                there = p1_r[it, k - 1, r].astype(F32)
                total += there
                lower += jnp.where(k <= a, 1.0, 0.0).astype(F32) * there
            pfx[m] = lower
            for k in (1, 2, 3):
                up = jnp.where(b + k < 4, 1.0, 0.0).astype(F32)
                p2_s[k - 1, r] = (on0 * total + on1 * (lower + up * chip_sum)).astype(BF16)

        loop(two)
        for k in (4, 6, 5):
            px_msg(it, k).start()
        for k in (4, 6, 5):
            px_msg(it, k).wait_recv()

        def three(r, m):
            p = pfx[m]
            for k in (1, 2, 3):
                keep = jnp.where(is0 & (k > b), 0.0, 1.0).astype(F32)
                p += keep * p2_r[it, k - 1, r].astype(F32)
            pe_s[r] = (p + on0 * tf[m]).astype(BF16)
            p += on1 * px_r[it, r].astype(F32) + first * cur[0, x, m].astype(F32)
            pfx[m] = p
            if it == 0:
                cur[1, x, m] = p.astype(BF16)

        loop(three)
        px_msg(it, 7).start()
        if it == 0:
            pfx_g.start(0, 3)
        px_msg(it, 7).wait_recv()

        def four(r, m):
            there = pl.ds(pl.multiple_of(64 - 64 * core + r.start, 16), 16)
            p = pe_r[it, r].astype(F32) + first * cur[0, x, there].astype(F32)
            pfx[there] = p
            if it == 0:
                cur[1, x, there] = p.astype(BF16)

        loop(four)
        if it == 0:
            pfx_g.start(2, 1)
        for m in range(8 + (it == ITERS - 1)):
            px_msg(it, m).wait_send()

    def slide():
        px_msg(ITERS - 1, 8).wait_recv()
        one = off_ref[0] == 1
        last = tm == 31

        def body(i, carry):
            rows = pl.ds(pl.multiple_of(16 * i, 16), 16)
            rows1 = pl.ds(pl.multiple_of(TOK + 16 * i, 16), 16)
            c1 = pfx[rows] + t[rows]
            c2 = c1 + t[rows1]
            c3 = c2 + sl_r[rows].astype(F32)
            c2 = jnp.where(last, c1, c2)
            c3 = jnp.where(last, c1, c3)
            out_ref[rows] = jnp.where(one, c1, c2).astype(BF16)
            out_ref[rows1] = jnp.where(one, c2, c3).astype(BF16)
            return carry

        lax.fori_loop(0, 8, body, 0)

    lat_g.start(0, 1, 2, 3)
    s0(0)
    s0(1)
    s0(2)
    s1(0)
    s2(0)
    swap_finish()
    s0(3)
    lat_g.forward()
    modulation()
    s1(1)
    s2(1)
    block_stats(0, x)
    lat_g.recv(2, 3)
    block_stats(0, x1)
    block_stats(0, x3)
    lat_g.recv(4, 5)
    block_stats(0, x2)
    norm(0)

    def weights(k, carry):
        s3(k)

        @pl.when(k < 2)
        def _():
            s1(k + 2)
            s2(k + 2)

        s5(k)
        s6(k)
        project(k)
        return carry

    lax.fori_loop(0, 3, weights, 0)
    attention(0)
    s3(3)
    hd_g[0].forward()
    s5(3)
    s6(3)
    out_project(0)
    terms(0)
    t0_g.start(0, 1, 2, 3)
    prefix(0)
    lax.fori_loop(0, 4, lambda k, c: (w_sent(k), c)[1], 0)
    lat_g.sent()
    hd_g[0].sent()
    t0_g.recv(2, 3, 4, 5)
    block_second(x)
    block_stats(1, x)
    pfx_g.forward()
    pfx_g.recv(2, 3)
    for q in (x1, x3):
        block_second(q)
        block_stats(1, q)
    pfx_g.recv(4, 5)
    block_second(x2)
    block_stats(1, x2)
    norm(1)
    lax.fori_loop(0, 3, lambda k, c: (project(k), c)[1], 0)
    attention(1)
    hd_g[1].forward()
    out_project(1)
    terms(1)
    prefix(1)
    slide()
    t0_g.sent()
    pfx_g.sent()
    hd_g[1].sent()


def features(step_index, mod_table):
    half = mod_table.shape[0] // 2
    freqs = jnp.exp(-math.log(10000.0) * jnp.arange(half).astype(F32) / half)
    angles = step_index.astype(F32)[:, None] * freqs[None, :]
    return jnp.concatenate([jnp.cos(angles), jnp.sin(angles)], axis=1).astype(BF16)


def per_device(latents, noise, mod_table, w_query, w_key, w_value, w_out, step_index, slide_offset):
    feats = features(step_index, mod_table)
    feats = jnp.concatenate([feats, jnp.zeros((14, feats.shape[1]), BF16)], axis=0)
    step_size = (step_index.astype(F32) + 1.0) / 2000.0
    hg = jnp.concatenate([step_size, 0.2 * jnp.sqrt(step_size)])
    hbm = pl.BlockSpec(memory_space=pl.ANY)
    vmem = pl.BlockSpec(memory_space=pltpu.VMEM)
    smem = pl.BlockSpec(memory_space=pltpu.SMEM)
    dma = pltpu.SemaphoreType.DMA
    out = pl.pallas_call(
        kernel,
        out_shape=jax.ShapeDtypeStruct((ROWS, QUART), BF16),
        in_specs=[hbm] * 7 + [vmem, smem, smem],
        out_specs=vmem,
        scratch_shapes=[
            pltpu.VMEM((4, WIDTH, HW), BF16),
            pltpu.VMEM((ITERS, 4, ROWS, QUART), BF16),
            pltpu.VMEM((4, ROWS, QUART), BF16),
            pltpu.VMEM((ROWS, HW), F32),
            pltpu.VMEM((3, ROWS, HW), BF16),
            pltpu.VMEM((ITERS, 4, ROWS, HW), BF16),
            pltpu.VMEM((4, ROWS, QUART), BF16),
            pltpu.VMEM((4, TOK, QUART), BF16),
            pltpu.VMEM((ROWS, QUART), F32),
            pltpu.VMEM((ROWS, QUART), BF16),
            pltpu.VMEM((9, 16, QUART), F32),
            pltpu.VMEM((4, 2, ROWS, 128), F32),
            pltpu.VMEM((TOK, QUART), F32),
            pltpu.VMEM((64, QUART), BF16),
            pltpu.VMEM((ITERS, 64, QUART), BF16),
            pltpu.VMEM((64, QUART), BF16),
            pltpu.VMEM((ITERS, 3, 64, QUART), BF16),
            pltpu.VMEM((3, 64, QUART), BF16),
            pltpu.VMEM((ITERS, 3, 64, QUART), BF16),
            pltpu.VMEM((64, QUART), BF16),
            pltpu.VMEM((ITERS, 64, QUART), BF16),
            pltpu.VMEM((TOK, QUART), F32),
            pltpu.VMEM((TOK, QUART), BF16),
            pltpu.VMEM((TOK, QUART), BF16),
            dma((6,)),
            dma((4, N_MSG)),
            dma((4, N_MSG)),
            dma((3, 6)),
            dma((3, 6)),
            dma((ITERS, 6)),
            dma((ITERS, 6)),
            dma((ITERS, 9)),
            dma((ITERS, 9)),
            dma,
            dma,
        ],
        compiler_params=pltpu.CompilerParams(
            collective_id=0, has_side_effects=True, vmem_limit_bytes=62 * 1024 * 1024
        ),
        cost_estimate=pl.CostEstimate(
            flops=2 * ITERS * 4 * ROWS * WIDTH * HW, bytes_accessed=12_000_000, transcendentals=0
        ),
    )(
        latents.reshape(ROWS, QUART), noise.reshape(ROWS, QUART), mod_table,
        w_query, w_key, w_value, w_out.T, feats, hg, slide_offset.reshape(1),
    )
    return out.reshape(latents.shape)


def solution(mesh):
    placed = (
        P("tm", None, "tp"),
        P("tm", None, "tp"),
        P(),
        P("tm", "tp"),
        P("tm", "tp"),
        P("tm", "tp"),
        P("tp", "tm"),
        P("tm"),
        P(),
    )
    return jax.shard_map(
        per_device, mesh=mesh, in_specs=placed, out_specs=P("tm", None, "tp"), check_vma=False
    )
```

```python
import functools
import math

import jax
import jax.numpy as jnp
from jax import lax
from jax.experimental import pallas as pl
from jax.experimental.pallas import tpu as pltpu
from jax.sharding import PartitionSpec as P

HEAD_SIZE = 128
HEADS = 5
ITERS = 2
TOK = 128
ROWS = 256
QUART = 1280
WIDTH = 5120
HW = 640
SHARD = 160
HALF = 80
MESH = pl.DeviceIdType.MESH
F32 = jnp.float32
BF16 = jnp.bfloat16
N_MSG = 36


def kernel(
    lat_ref, noise_ref, table_ref, wq_ref, wk_ref, wv_ref, wo_ref, feats_ref, hg_ref,
    out_ref,
    w, cur, y, acc, qkv, hda, hdb, part, tb, t, nz, mods, stat,
    tf, px_s, px_r, p1_s, p1_r, p2_s, p2_r, pe_s, pe_r, pfx, sl_s, sl_r,
    loc_sem, w_ss, w_rs, ag_ss, ag_rs, hd_ss, hd_rs, px_ss, px_rs, tr_ss, tr_rs,
):
    tm = lax.axis_index("tm")
    x = lax.axis_index("tp")
    core = lax.rem(tm, 2)
    chip = lax.div(tm, 2)
    yy, zz = lax.div(chip, 4), lax.rem(chip, 4)
    is0 = core == 0
    a = jnp.where(is0, zz, yy)
    b = jnp.where(is0, yy, zz)

    def rank(da, db):
        aa, bb = lax.rem(a + da, 4), lax.rem(b + db, 4)
        return jnp.where(is0, bb * 4 + aa, aa * 4 + bb) * 2 + core

    def dev(da, db):
        return (rank(da, db), x)

    sib = (tm + 1 - 2 * core, x)
    xp = (tm, lax.rem(x + 1, 4))
    xm = (tm, lax.rem(x + 3, 4))
    following = (lax.rem(tm + 1, 32), x)
    before = (lax.rem(tm + 31, 32), x)
    swapped = ((x * 4 + zz) * 2 + core, yy)
    swaps = x != yy
    x1, x2, x3 = lax.rem(x + 1, 4), lax.rem(x + 2, 4), lax.rem(x + 3, 4)

    def remote(src, dst, ss, rs, to):
        return pltpu.make_async_remote_copy(
            src_ref=src, dst_ref=dst, send_sem=ss, recv_sem=rs, device_id=to, device_id_type=MESH
        )

    own = pl.ds(pl.multiple_of(SHARD * tm, 16), SHARD)
    local = [
        pltpu.make_async_copy(src, w.at[k, own], loc_sem.at[k])
        for k, src in enumerate((wq_ref, wk_ref, wv_ref))
    ]
    local.append(pltpu.make_async_copy(lat_ref, cur.at[0, x], loc_sem.at[4]))
    local.append(pltpu.make_async_copy(noise_ref, nz, loc_sem.at[5]))
    for c in local:
        c.start()

    barrier = pltpu.get_barrier_semaphore()
    peers = [sib, xp, xm, following, before]
    peers += [dev(k, 0) for k in (1, 2, 3)] + [dev(0, k) for k in (1, 2, 3)]
    for peer in peers:
        pl.semaphore_signal(barrier, inc=1, device_id=peer, device_id_type=MESH)

    @pl.when(swaps)
    def _():
        pl.semaphore_signal(barrier, inc=1, device_id=swapped, device_id_type=MESH)

    pl.semaphore_wait(barrier, len(peers) + jnp.where(swaps, 1, 0))

    def swap_msg():
        there = pl.ds(pl.multiple_of(SHARD * swapped[0], 16), SHARD)
        return remote(wo_ref, w.at[3, there], tr_ss, tr_rs, swapped)

    def swap_local():
        return pltpu.make_async_copy(wo_ref, w.at[3, own], loc_sem.at[6])

    def swap_start():
        @pl.when(swaps)
        def _():
            swap_msg().start()

        @pl.when(jnp.logical_not(swaps))
        def _():
            swap_local().start()

    def swap_finish():
        @pl.when(swaps)
        def _():
            swap_msg().wait()

        @pl.when(jnp.logical_not(swaps))
        def _():
            swap_local().wait()

    for c in local:
        c.wait()

    class Gather:
        def __init__(self, block, halves, ss, rs):
            self.block, self.halves, self.ss, self.rs = block, halves, ss, rs

        def msg(self, m):
            to = xp if m in (0, 2, 4) else xm
            src = (x, x, x, x, x3, x1)[m]
            ref = self.block(src, self.halves[(0, 1, 1, 0, 0, 1)[m]])
            return remote(ref, ref, self.ss(m), self.rs(m), to)

        def start(self, *ms):
            for m in ms:
                self.msg(m).start()

        def forward(self):
            self.msg(0).wait_recv()
            self.msg(4).start()
            self.msg(1).wait_recv()
            self.msg(5).start()

        def recv(self, *ms):
            for m in ms:
                self.msg(m).wait_recv()

        def sent(self):
            for m in range(6):
                self.msg(m).wait_send()

    steps = (pl.ds(0, TOK), pl.ds(TOK, TOK))
    lat_g = Gather(lambda q, r: cur.at[0, q, r], steps, lambda m: ag_ss.at[0, m], lambda m: ag_rs.at[0, m])
    t0_g = Gather(
        lambda q, r: tb.at[q, r], (pl.ds(0, 64), pl.ds(64, 64)),
        lambda m: ag_ss.at[1, m], lambda m: ag_rs.at[1, m],
    )
    pfx_g = Gather(
        lambda q, r: cur.at[1, q, r],
        (pl.ds(pl.multiple_of(64 * core, 64), 64), pl.ds(pl.multiple_of(64 - 64 * core, 64), 64)),
        lambda m: ag_ss.at[2, m], lambda m: ag_rs.at[2, m],
    )
    hd = (hda, hdb)
    blocks = (pl.ds(0, 256), pl.ds(256, 384))
    block_heads = ((0, 1), (2, 3, 4))

    def hd_gather(it, c):
        return Gather(
            lambda q, r: hd[c].at[it, q, r], steps,
            lambda m: hd_ss.at[it, c, m], lambda m: hd_rs.at[it, c, m],
        )

    hd_g = [[hd_gather(it, c) for c in range(2)] for it in range(ITERS)]

    def rows_of(r, lo, n):
        return pl.ds(pl.multiple_of(SHARD * r + lo, 16), n)

    def w_msg(k, m):
        if m < 4:
            ref = (
                w.at[k, rows_of(tm, 0, SHARD)],
                w.at[k, rows_of(tm, 0, SHARD)],
                w.at[k, rows_of(rank(3, 0), 0, HALF)],
                w.at[k, rows_of(rank(1, 0), HALF, HALF)],
            )[m]
            to = dev(1, 0) if m in (0, 2) else dev(3, 0)
        elif m < 20:
            j, i = divmod(m - 4, 4)
            da = (0, 3, 1, 2)[j]
            ref = (
                w.at[k, rows_of(rank(da, 0), 0, SHARD)],
                w.at[k, rows_of(rank(da, 0), 0, SHARD)],
                w.at[k, rows_of(rank(da, 3), 0, HALF)],
                w.at[k, rows_of(rank(da, 1), HALF, HALF)],
            )[i]
            to = dev(0, 1) if i in (0, 2) else dev(0, 3)
        else:
            j, i = divmod(m - 20, 4)
            ref = w.at[k, rows_of(rank((0, 3, 1, 2)[j], (0, 3, 1, 2)[i]), 0, SHARD)]
            to = sib
        return remote(ref, ref, w_ss.at[k, m], w_rs.at[k, m], to)

    def w_start(k, *ms):
        for m in ms:
            w_msg(k, m).start()

    def w_recv(k, *ms):
        for m in ms:
            w_msg(k, m).wait_recv()

    def s0(k):
        w_start(k, 0, 1, 4, 5, 20)

    def s1(k):
        w_recv(k, 0)
        w_start(k, 2, 8, 9, 24)
        w_recv(k, 1)
        w_start(k, 3, 12, 13, 28)

    def s2(k):
        w_recv(k, 2, 3)
        w_start(k, 16, 17, 32)

    def s3(k, parts=(0, 1, 2, 3)):
        for j in parts:
            w_recv(k, 4 + 4 * j)
            w_start(k, 6 + 4 * j, 21 + 4 * j)
            w_recv(k, 5 + 4 * j)
            w_start(k, 7 + 4 * j, 22 + 4 * j)

    def s5(k):
        for j in range(4):
            w_recv(k, 6 + 4 * j, 7 + 4 * j)
            w_start(k, 23 + 4 * j)

    def s6(k):
        for m in range(20, 36):
            w_msg(k, m).wait_recv()

    def w_sent(k):
        for m in range(N_MSG):
            w_msg(k, m).wait_send()

    def modulation():
        for base in (0, 4, 8):
            count = 4 if base < 8 else 1
            for k in range(count):
                start = (base + k) * QUART if base < 8 else 2 * WIDTH + x * QUART
                pltpu.make_async_copy(
                    table_ref.at[:, pl.ds(pl.multiple_of(start, 128), QUART)],
                    part.at[k], loc_sem.at[k],
                ).start()
            for k in range(count):
                pltpu.make_async_copy(
                    table_ref.at[:, pl.ds(0, QUART)], part.at[k], loc_sem.at[k]
                ).wait()
                mods[base + k] = jnp.dot(feats_ref[...], part[k], preferred_element_type=F32)

    def block_stats(it, q):
        def body(i, carry):
            rows = pl.ds(pl.multiple_of(32 * i, 32), 32)
            c = cur[it, q, rows].astype(F32)
            mean = jnp.sum(c, axis=-1, keepdims=True) / QUART
            d = c - mean
            stat[q, 0, rows] = jnp.broadcast_to(mean, (32, 128))
            stat[q, 1, rows] = jnp.broadcast_to(jnp.sum(d * d, axis=-1, keepdims=True), (32, 128))
            return carry

        lax.fori_loop(0, 8, body, 0)

    def block_second(q):
        def body(i, carry):
            rows = pl.ds(pl.multiple_of(16 * i, 16), 16)
            rows1 = pl.ds(pl.multiple_of(TOK + 16 * i, 16), 16)
            cur[1, q, rows1] = (cur[1, q, rows].astype(F32) + tb[q, rows].astype(F32)).astype(BF16)
            return carry

        lax.fori_loop(0, 8, body, 0)

    def norm(it):
        def body(i, carry):
            rows = pl.ds(pl.multiple_of(32 * i, 32), 32)
            step = lax.div(i, 4)
            means = [stat[q, 0, rows] for q in range(4)]
            mean = (means[0] + means[1] + means[2] + means[3]) * 0.25
            square = jnp.zeros((32, 128), F32)
            for q in range(4):
                off = means[q] - mean
                square += stat[q, 1, rows] + QUART * off * off
            inv = lax.rsqrt(square / WIDTH + 1e-6)
            for q in range(4):
                for c in range(5):
                    cols = pl.ds(256 * c, 256)
                    m2 = jnp.concatenate([mean, mean], axis=1)
                    i2 = jnp.concatenate([inv, inv], axis=1)
                    d = (cur[it, q, rows, cols].astype(F32) - m2) * i2
                    shift = mods[q, pl.ds(step, 1), cols]
                    scale = mods[4 + q, pl.ds(step, 1), cols]
                    y[q, rows, cols] = (d * (1.0 + scale) + shift).astype(BF16)
            return carry

        lax.fori_loop(0, 8, body, 0)

    def project(k):
        def body(q, carry):
            rows = pl.ds(pl.multiple_of(q * QUART, 128), QUART)
            acc[...] += jnp.dot(y[q], w[k, rows], preferred_element_type=F32)
            return carry

        acc[...] = jnp.zeros_like(acc)
        lax.fori_loop(0, 4, body, 0)
        qkv[k] = acc[...].astype(BF16)

    def project_block(c):
        cols = blocks[c]

        def body(k, carry):
            total = None
            for q in range(4):
                new = jnp.dot(
                    y[q], w[k, pl.ds(q * QUART, QUART), cols], preferred_element_type=F32
                )
                total = new if total is None else total + new
            qkv[k, :, cols] = total.astype(BF16)
            return carry

        lax.fori_loop(0, 3, body, 0)

    def attention_block(it, c):
        for step in range(2):
            for n, h in enumerate(block_heads[c]):
                rows, cols = pl.ds(TOK * step, TOK), pl.ds(HEAD_SIZE * h, HEAD_SIZE)
                s = lax.dot_general(
                    qkv[0, rows, cols], qkv[1, rows, cols], (((1,), (1,)), ((), ())),
                    preferred_element_type=F32,
                ) * (1.0 / math.sqrt(HEAD_SIZE))
                e = jnp.exp(s - jnp.max(s, axis=-1, keepdims=True))
                p = (e / jnp.sum(e, axis=-1, keepdims=True)).astype(BF16)
                hd[c][it, x, rows, HEAD_SIZE * n : HEAD_SIZE * (n + 1)] = jnp.dot(
                    p, qkv[2, rows, cols], preferred_element_type=F32
                ).astype(BF16)
        hd_g[it][c].start(0, 3, 1, 2)

    def attention(it):
        for c in range(2):
            attention_block(it, c)

    def out_part(it, q, add):
        def body(i, carry):
            rows = pl.ds(pl.multiple_of(q * QUART + i * 256, 128), 256)
            cols = pl.ds(pl.multiple_of(i * 256, 128), 256)
            new = None
            for c in range(2):
                term = lax.dot_general(
                    hd[c][it, q], w[3, rows, blocks[c]], (((1,), (1,)), ((), ())),
                    preferred_element_type=F32,
                )
                new = term if new is None else new + term
            t[:, cols] = t[:, cols] + new if add else new
            return carry

        lax.fori_loop(0, 5, body, 0)

    def out_project(it):
        out_part(it, x, False)
        for g in hd_g[it]:
            g.recv(2)
        out_part(it, x3, True)
        for g in hd_g[it]:
            g.recv(3)
        out_part(it, x1, True)
        for g in hd_g[it]:
            g.recv(4, 5)
        out_part(it, x2, True)

    def hd_sent(it):
        for g in hd_g[it]:
            g.sent()

    first = jnp.where(tm == 0, 1.0, 0.0).astype(F32)

    def terms(it):
        def body(i, carry):
            rows = pl.ds(pl.multiple_of(16 * i, 16), 16)
            step = lax.div(i, 8)
            gate = mods[8, pl.ds(step, 1)] * hg_ref[step]
            t[rows] = gate * t[rows] + hg_ref[2 + step] * nz[rows].astype(F32)
            return carry

        lax.fori_loop(0, 16, body, 0)

        def body2(i, carry):
            rows = pl.ds(pl.multiple_of(16 * i, 16), 16)
            rows1 = pl.ds(pl.multiple_of(TOK + 16 * i, 16), 16)
            t0 = t[rows]
            tf[rows] = t0 + t[rows1] + first * cur[0, x, rows].astype(F32)
            if it == 0:
                tb[x, rows] = t0.astype(BF16)
            return carry

        lax.fori_loop(0, 8, body2, 0)

    mine = pl.ds(pl.multiple_of(64 * core, 64), 64)
    other = pl.ds(pl.multiple_of(64 - 64 * core, 64), 64)
    on0 = jnp.where(is0, 1.0, 0.0).astype(F32)
    on1 = 1.0 - on0

    def px_msg(it, m):
        if m == 0:
            src, dst, to = px_s, px_r.at[it], sib
        elif m < 4:
            src, dst, to = p1_s, p1_r.at[it, m - 1], dev(m, 0)
        elif m < 7:
            src, dst, to = p2_s.at[m - 4], p2_r.at[it, m - 4], dev(0, m - 3)
        elif m == 7:
            src, dst, to = pe_s, pe_r.at[it], sib
        else:
            src, dst, to = sl_s, sl_r, before
        return remote(src, dst, px_ss.at[it, m], px_rs.at[it, m], to)

    def prefix(it):
        px_s[...] = tf[other].astype(BF16)
        px_msg(it, 0).start()
        if it == ITERS - 1:
            sl_s[...] = t[0:TOK].astype(BF16)
            px_msg(it, 8).start()
        px_msg(it, 0).wait_recv()

        def loop(f):
            def body(i, carry):
                f(pl.ds(pl.multiple_of(16 * i, 16), 16),
                  pl.ds(pl.multiple_of(64 * core + 16 * i, 16), 16))
                return carry

            lax.fori_loop(0, 4, body, 0)

        def one(r, m):
            p1_s[r] = (tf[m] + px_r[it, r].astype(F32)).astype(BF16)

        loop(one)
        for k in (1, 3, 2):
            px_msg(it, k).start()
        for k in (1, 3, 2):
            px_msg(it, k).wait_recv()
        if it == 0:
            t0_g.forward()

        def two(r, m):
            chip_sum = tf[m] + px_r[it, r].astype(F32)
            lower = jnp.zeros((16, QUART), F32)
            total = chip_sum
            for k in (1, 2, 3):
                there = p1_r[it, k - 1, r].astype(F32)
                total += there
                lower += jnp.where(k <= a, 1.0, 0.0).astype(F32) * there
            pfx[m] = lower
            for k in (1, 2, 3):
                up = jnp.where(b + k < 4, 1.0, 0.0).astype(F32)
                p2_s[k - 1, r] = (on0 * total + on1 * (lower + up * chip_sum)).astype(BF16)

        loop(two)
        for k in (4, 6, 5):
            px_msg(it, k).start()
        for k in (4, 6, 5):
            px_msg(it, k).wait_recv()

        def three(r, m):
            p = pfx[m]
            for k in (1, 2, 3):
                keep = jnp.where(is0 & (k > b), 0.0, 1.0).astype(F32)
                p += keep * p2_r[it, k - 1, r].astype(F32)
            pe_s[r] = (p + on0 * tf[m]).astype(BF16)
            p += on1 * px_r[it, r].astype(F32) + first * cur[0, x, m].astype(F32)
            pfx[m] = p
            if it == 0:
                cur[1, x, m] = p.astype(BF16)

        loop(three)
        px_msg(it, 7).start()
        if it == 0:
            pfx_g.start(0, 3)
        px_msg(it, 7).wait_recv()

        def four(r, m):
            there = pl.ds(pl.multiple_of(64 - 64 * core + r.start, 16), 16)
            p = pe_r[it, r].astype(F32) + first * cur[0, x, there].astype(F32)
            pfx[there] = p
            if it == 0:
                cur[1, x, there] = p.astype(BF16)

        loop(four)
        if it == 0:
            pfx_g.start(2, 1)
        for m in range(8 + (it == ITERS - 1)):
            px_msg(it, m).wait_send()

    def slide():
        px_msg(ITERS - 1, 8).wait_recv()
        last = tm == 31

        def body(i, carry):
            rows = pl.ds(pl.multiple_of(16 * i, 16), 16)
            rows1 = pl.ds(pl.multiple_of(TOK + 16 * i, 16), 16)
            rows2 = pl.ds(pl.multiple_of(2 * TOK + 16 * i, 16), 16)
            c1 = pfx[rows] + t[rows]
            c2 = c1 + t[rows1]
            c3 = c2 + sl_r[rows].astype(F32)
            c2 = jnp.where(last, c1, c2)
            c3 = jnp.where(last, c1, c3)
            out_ref[rows] = c1.astype(BF16)
            out_ref[rows1] = c2.astype(BF16)
            out_ref[rows2] = c3.astype(BF16)
            return carry

        lax.fori_loop(0, 8, body, 0)

    swap_start()
    lat_g.start(0, 1, 2, 3)
    s0(0)
    s0(1)
    s1(0)
    s2(0)
    s0(2)
    s1(1)
    s2(1)
    lat_g.forward()
    s3(0)
    s1(2)
    s2(2)
    modulation()
    s3(1)
    s5(0)
    swap_finish()
    s0(3)
    block_stats(0, x)
    lat_g.recv(2, 3)
    block_stats(0, x1)
    block_stats(0, x3)
    lat_g.recv(4, 5)
    block_stats(0, x2)
    norm(0)
    s6(0)
    project(0)
    s3(2)
    s5(1)
    s1(3)
    s2(3)
    s6(1)
    project(1)
    s3(3, (0,))
    s5(2)
    s3(3, (1, 2))
    s6(2)
    project(2)
    attention(0)
    s3(3, (3,))
    for g in hd_g[0]:
        g.forward()
    s5(3)
    s6(3)
    out_project(0)
    terms(0)
    t0_g.start(0, 1, 2, 3)
    prefix(0)
    pfx_g.forward()
    t0_g.recv(2, 3, 4, 5)
    block_second(x)
    block_stats(1, x)
    pfx_g.recv(2, 3)
    for q in (x1, x3):
        block_second(q)
        block_stats(1, q)
    pfx_g.recv(4, 5)
    block_second(x2)
    block_stats(1, x2)
    norm(1)
    project_block(0)
    attention_block(1, 0)
    project_block(1)
    hd_g[1][0].forward()
    attention_block(1, 1)
    hd_g[1][1].forward()
    out_project(1)
    terms(1)
    prefix(1)
    slide()
    lax.fori_loop(0, 4, lambda k, c: (w_sent(k), c)[1], 0)
    lat_g.sent()
    t0_g.sent()
    pfx_g.sent()
    hd_sent(0)
    hd_sent(1)


def features(step_index, mod_table):
    half = mod_table.shape[0] // 2
    freqs = jnp.exp(-math.log(10000.0) * jnp.arange(half).astype(F32) / half)
    angles = step_index.astype(F32)[:, None] * freqs[None, :]
    return jnp.concatenate([jnp.cos(angles), jnp.sin(angles)], axis=1).astype(BF16)


def per_device(latents, noise, mod_table, w_query, w_key, w_value, w_out, step_index, slide_offset):
    feats = features(step_index, mod_table)
    feats = jnp.concatenate([feats, jnp.zeros((14, feats.shape[1]), BF16)], axis=0)
    step_size = (step_index.astype(F32) + 1.0) / 2000.0
    hg = jnp.concatenate([step_size, 0.2 * jnp.sqrt(step_size)])
    hbm = pl.BlockSpec(memory_space=pl.ANY)
    vmem = pl.BlockSpec(memory_space=pltpu.VMEM)
    smem = pl.BlockSpec(memory_space=pltpu.SMEM)
    dma = pltpu.SemaphoreType.DMA
    out = pl.pallas_call(
        kernel,
        out_shape=jax.ShapeDtypeStruct((3 * TOK, QUART), BF16),
        in_specs=[hbm] * 7 + [vmem, smem],
        out_specs=vmem,
        scratch_shapes=[
            pltpu.VMEM((4, WIDTH, HW), BF16),
            pltpu.VMEM((ITERS, 4, ROWS, QUART), BF16),
            pltpu.VMEM((4, ROWS, QUART), BF16),
            pltpu.VMEM((ROWS, HW), F32),
            pltpu.VMEM((3, ROWS, HW), BF16),
            pltpu.VMEM((ITERS, 4, ROWS, 256), BF16),
            pltpu.VMEM((ITERS, 4, ROWS, 384), BF16),
            pltpu.VMEM((4, ROWS, QUART), BF16),
            pltpu.VMEM((4, TOK, QUART), BF16),
            pltpu.VMEM((ROWS, QUART), F32),
            pltpu.VMEM((ROWS, QUART), BF16),
            pltpu.VMEM((9, 16, QUART), F32),
            pltpu.VMEM((4, 2, ROWS, 128), F32),
            pltpu.VMEM((TOK, QUART), F32),
            pltpu.VMEM((64, QUART), BF16),
            pltpu.VMEM((ITERS, 64, QUART), BF16),
            pltpu.VMEM((64, QUART), BF16),
            pltpu.VMEM((ITERS, 3, 64, QUART), BF16),
            pltpu.VMEM((3, 64, QUART), BF16),
            pltpu.VMEM((ITERS, 3, 64, QUART), BF16),
            pltpu.VMEM((64, QUART), BF16),
            pltpu.VMEM((ITERS, 64, QUART), BF16),
            pltpu.VMEM((TOK, QUART), F32),
            pltpu.VMEM((TOK, QUART), BF16),
            pltpu.VMEM((TOK, QUART), BF16),
            dma((7,)),
            dma((4, N_MSG)),
            dma((4, N_MSG)),
            dma((3, 6)),
            dma((3, 6)),
            dma((ITERS, 2, 6)),
            dma((ITERS, 2, 6)),
            dma((ITERS, 9)),
            dma((ITERS, 9)),
            dma,
            dma,
        ],
        compiler_params=pltpu.CompilerParams(
            collective_id=0, has_side_effects=True, vmem_limit_bytes=62 * 1024 * 1024
        ),
        cost_estimate=pl.CostEstimate(
            flops=2 * ITERS * 4 * ROWS * WIDTH * HW, bytes_accessed=12_000_000, transcendentals=0
        ),
    )(
        latents.reshape(ROWS, QUART), noise.reshape(ROWS, QUART), mod_table,
        w_query, w_key, w_value, w_out.T, feats, hg,
    )
    return lax.dynamic_slice_in_dim(out.reshape(3, TOK, QUART), slide_offset - 1, 2, 0)


def solution(mesh):
    placed = (
        P("tm", None, "tp"),
        P("tm", None, "tp"),
        P(),
        P("tm", "tp"),
        P("tm", "tp"),
        P("tm", "tp"),
        P("tp", "tm"),
        P("tm"),
        P(),
    )
    return jax.shard_map(
        per_device, mesh=mesh, in_specs=placed, out_specs=P("tm", None, "tp"), check_vma=False
    )
```

```python
import functools
import math

import jax
import jax.numpy as jnp
from jax import lax
from jax.experimental import pallas as pl
from jax.experimental.pallas import tpu as pltpu
from jax.sharding import PartitionSpec as P

HEAD_SIZE = 128
HEADS = 5
ITERS = 2
TOK = 128
ROWS = 256
QUART = 1280
WIDTH = 5120
HW = 640
SHARD = 160
HALF = 80
MESH = pl.DeviceIdType.MESH
F32 = jnp.float32
BF16 = jnp.bfloat16
N_MSG = 36


def kernel(
    lat_ref, noise_ref, table_ref, wq_ref, wk_ref, wv_ref, wo_ref, feats_ref, hg_ref,
    out_ref,
    w, cur, y, acc, uv, qkv, hda, hdb, part, tb, t, nz, mods, stat,
    tf, px_s, px_r, p1_s, p1_r, p2_s, p2_r, pe_s, pe_r, pfx, sl_s, sl_r,
    loc_sem, w_ss, w_rs, ag_ss, ag_rs, hd_ss, hd_rs, px_ss, px_rs, a_ss, a_rs, tr_ss, tr_rs,
):
    tm = lax.axis_index("tm")
    x = lax.axis_index("tp")
    core = lax.rem(tm, 2)
    chip = lax.div(tm, 2)
    yy, zz = lax.div(chip, 4), lax.rem(chip, 4)
    is0 = core == 0
    a = jnp.where(is0, zz, yy)
    b = jnp.where(is0, yy, zz)

    def rank(da, db):
        aa, bb = lax.rem(a + da, 4), lax.rem(b + db, 4)
        return jnp.where(is0, bb * 4 + aa, aa * 4 + bb) * 2 + core

    def dev(da, db):
        return (rank(da, db), x)

    sib = (tm + 1 - 2 * core, x)
    xp = (tm, lax.rem(x + 1, 4))
    xm = (tm, lax.rem(x + 3, 4))
    following = (lax.rem(tm + 1, 32), x)
    before = (lax.rem(tm + 31, 32), x)
    swapped = ((x * 4 + zz) * 2 + core, yy)
    swaps = x != yy
    x1, x2, x3 = lax.rem(x + 1, 4), lax.rem(x + 2, 4), lax.rem(x + 3, 4)

    def remote(src, dst, ss, rs, to):
        return pltpu.make_async_remote_copy(
            src_ref=src, dst_ref=dst, send_sem=ss, recv_sem=rs, device_id=to, device_id_type=MESH
        )

    own = pl.ds(pl.multiple_of(SHARD * tm, 16), SHARD)
    local = [
        pltpu.make_async_copy(src, w.at[k, own], loc_sem.at[k])
        for k, src in enumerate((wq_ref, wk_ref, wv_ref))
    ]
    local.append(pltpu.make_async_copy(lat_ref, cur.at[0, x], loc_sem.at[4]))
    local.append(pltpu.make_async_copy(noise_ref, nz, loc_sem.at[5]))
    for c in local:
        c.start()

    barrier = pltpu.get_barrier_semaphore()
    peers = [sib, xp, xm, following, before]
    peers += [(2 * lax.rem(chip + d, 16) + core, x) for d in range(1, 16)]
    for peer in peers:
        pl.semaphore_signal(barrier, inc=1, device_id=peer, device_id_type=MESH)

    @pl.when(swaps)
    def _():
        pl.semaphore_signal(barrier, inc=1, device_id=swapped, device_id_type=MESH)

    pl.semaphore_wait(barrier, len(peers) + jnp.where(swaps, 1, 0))

    def swap_msg():
        there = pl.ds(pl.multiple_of(SHARD * swapped[0], 16), SHARD)
        return remote(wo_ref, w.at[3, there], tr_ss, tr_rs, swapped)

    def swap_local():
        return pltpu.make_async_copy(wo_ref, w.at[3, own], loc_sem.at[6])

    def swap_start():
        @pl.when(swaps)
        def _():
            swap_msg().start()

        @pl.when(jnp.logical_not(swaps))
        def _():
            swap_local().start()

    def swap_finish():
        @pl.when(swaps)
        def _():
            swap_msg().wait()

        @pl.when(jnp.logical_not(swaps))
        def _():
            swap_local().wait()

    for c in local:
        c.wait()

    class Gather:
        def __init__(self, block, halves, ss, rs):
            self.block, self.halves, self.ss, self.rs = block, halves, ss, rs

        def msg(self, m):
            to = xp if m in (0, 2, 4) else xm
            src = (x, x, x, x, x3, x1)[m]
            ref = self.block(src, self.halves[(0, 1, 1, 0, 0, 1)[m]])
            return remote(ref, ref, self.ss(m), self.rs(m), to)

        def start(self, *ms):
            for m in ms:
                self.msg(m).start()

        def forward(self):
            self.msg(0).wait_recv()
            self.msg(4).start()
            self.msg(1).wait_recv()
            self.msg(5).start()

        def recv(self, *ms):
            for m in ms:
                self.msg(m).wait_recv()

        def sent(self):
            for m in range(6):
                self.msg(m).wait_send()

    steps = (pl.ds(0, TOK), pl.ds(TOK, TOK))
    lat_g = Gather(lambda q, r: cur.at[0, q, r], steps, lambda m: ag_ss.at[0, m], lambda m: ag_rs.at[0, m])
    t0_g = Gather(
        lambda q, r: tb.at[q, r], (pl.ds(0, 64), pl.ds(64, 64)),
        lambda m: ag_ss.at[1, m], lambda m: ag_rs.at[1, m],
    )
    pfx_g = Gather(
        lambda q, r: cur.at[1, q, r],
        (pl.ds(pl.multiple_of(64 * core, 64), 64), pl.ds(pl.multiple_of(64 - 64 * core, 64), 64)),
        lambda m: ag_ss.at[2, m], lambda m: ag_rs.at[2, m],
    )
    hd = (hda, hdb)
    blocks = (pl.ds(0, 256), pl.ds(256, 384))
    block_heads = ((0, 1), (2, 3, 4))
    whole = pl.ds(0, HW)

    def hd_gather(it, c):
        return Gather(
            lambda q, r: hd[c].at[it, q, r], steps,
            lambda m: hd_ss.at[it, c, m], lambda m: hd_rs.at[it, c, m],
        )

    hd_g = [[hd_gather(it, c) for c in range(2)] for it in range(ITERS)]

    def rows_of(r, lo, n):
        return pl.ds(pl.multiple_of(SHARD * r + lo, 16), n)

    def w_msg(k, m):
        if m < 4:
            ref = (
                w.at[k, rows_of(tm, 0, SHARD)],
                w.at[k, rows_of(tm, 0, SHARD)],
                w.at[k, rows_of(rank(3, 0), 0, HALF)],
                w.at[k, rows_of(rank(1, 0), HALF, HALF)],
            )[m]
            to = dev(1, 0) if m in (0, 2) else dev(3, 0)
        elif m < 20:
            j, i = divmod(m - 4, 4)
            da = (0, 3, 1, 2)[j]
            ref = (
                w.at[k, rows_of(rank(da, 0), 0, SHARD)],
                w.at[k, rows_of(rank(da, 0), 0, SHARD)],
                w.at[k, rows_of(rank(da, 3), 0, HALF)],
                w.at[k, rows_of(rank(da, 1), HALF, HALF)],
            )[i]
            to = dev(0, 1) if i in (0, 2) else dev(0, 3)
        else:
            j, i = divmod(m - 20, 4)
            ref = w.at[k, rows_of(rank((0, 3, 1, 2)[j], (0, 3, 1, 2)[i]), 0, SHARD)]
            to = sib
        return remote(ref, ref, w_ss.at[k, m], w_rs.at[k, m], to)

    def w_start(k, *ms):
        for m in ms:
            w_msg(k, m).start()

    def w_recv(k, *ms):
        for m in ms:
            w_msg(k, m).wait_recv()

    def s0(k):
        w_start(k, 0, 1, 4, 5, 20)

    def s1(k):
        w_recv(k, 0)
        w_start(k, 2, 8, 9, 24)
        w_recv(k, 1)
        w_start(k, 3, 12, 13, 28)

    def s2(k):
        w_recv(k, 2, 3)
        w_start(k, 16, 17, 32)

    def s3(k, parts=(0, 1, 2, 3)):
        for j in parts:
            w_recv(k, 4 + 4 * j)
            w_start(k, 6 + 4 * j, 21 + 4 * j)
            w_recv(k, 5 + 4 * j)
            w_start(k, 7 + 4 * j, 22 + 4 * j)

    def s5(k):
        for j in range(4):
            w_recv(k, 6 + 4 * j, 7 + 4 * j)
            w_start(k, 23 + 4 * j)

    def s6(k):
        for m in range(20, 36):
            w_msg(k, m).wait_recv()

    def w_sent(k):
        for m in range(N_MSG):
            w_msg(k, m).wait_send()

    def modulation():
        for base in (0, 4, 8):
            count = 4 if base < 8 else 1
            for k in range(count):
                start = (base + k) * QUART if base < 8 else 2 * WIDTH + x * QUART
                pltpu.make_async_copy(
                    table_ref.at[:, pl.ds(pl.multiple_of(start, 128), QUART)],
                    part.at[k], loc_sem.at[k],
                ).start()
            for k in range(count):
                pltpu.make_async_copy(
                    table_ref.at[:, pl.ds(0, QUART)], part.at[k], loc_sem.at[k]
                ).wait()
                mods[base + k] = jnp.dot(feats_ref[...], part[k], preferred_element_type=F32)
        row = lax.broadcasted_iota(jnp.int32, (16, QUART), 0)
        for q in range(4):
            rows = jnp.where(row < 2, 1.0 + mods[4 + q], jnp.where(row < 4, mods[q], 0.0))
            y[q, ROWS : ROWS + 16] = rows.astype(BF16)

    def block_stats(it, q):
        def body(i, carry):
            rows = pl.ds(pl.multiple_of(32 * i, 32), 32)
            c = cur[it, q, rows].astype(F32)
            mean = jnp.sum(c, axis=-1, keepdims=True) / QUART
            d = c - mean
            stat[q, 0, rows] = jnp.broadcast_to(mean, (32, 128))
            stat[q, 1, rows] = jnp.broadcast_to(jnp.sum(d * d, axis=-1, keepdims=True), (32, 128))
            return carry

        lax.fori_loop(0, 8, body, 0)

    def prepare(q):
        def body(i, carry):
            rows = pl.ds(pl.multiple_of(32 * i, 32), 32)
            p = cur[1, q, rows].astype(F32)
            for step in range(2):
                here = pl.ds(pl.multiple_of(TOK * step + 32 * i, 32), 32)
                c = p if step == 0 else p + tb[q, rows].astype(F32)
                mean = jnp.sum(c, axis=-1, keepdims=True) / QUART
                d = c - mean
                stat[q, 0, here] = jnp.broadcast_to(mean, (32, 128))
                stat[q, 1, here] = jnp.broadcast_to(
                    jnp.sum(d * d, axis=-1, keepdims=True), (32, 128)
                )
                y[q, here] = (d * (1.0 + mods[4 + q, step : step + 1])).astype(BF16)
            return carry

        lax.fori_loop(0, 4, body, 0)

    def block_project(q, cols, first=False):
        rows = pl.ds(pl.multiple_of(q * QUART, 128), QUART)

        def body(k, carry):
            new = jnp.dot(y[q, 0:ROWS], w[k, rows, cols], preferred_element_type=F32)
            acc[k, :, cols] = new if first else acc[k, :, cols] + new
            return carry

        lax.fori_loop(0, 3, body, 0)

    def finalize(c):
        def body(step, i, carry):
            rows = pl.ds(pl.multiple_of(TOK * step + 32 * i, 32), 32)
            means = [stat[q, 0, rows] for q in range(4)]
            mean = (means[0] + means[1] + means[2] + means[3]) * 0.25
            offs = [m - mean for m in means]
            square = jnp.zeros((32, 128), F32)
            for q in range(4):
                square += stat[q, 1, rows] + QUART * offs[q] * offs[q]
            inv = lax.rsqrt(square / WIDTH + 1e-6)
            for k in range(3):
                for h in block_heads[c]:
                    cols = pl.ds(HEAD_SIZE * h, HEAD_SIZE)
                    value = acc[k, rows, cols]
                    add = jnp.zeros((1, HEAD_SIZE), F32)
                    for q in range(4):
                        value += offs[q] * uv[k, q, step : step + 1, cols]
                        add += uv[k, q, 2 + step : 3 + step, cols]
                    qkv[k, rows, cols] = (inv * value + add).astype(BF16)
            return carry

        for step in range(2):
            lax.fori_loop(0, 4, functools.partial(body, step), 0)

    def norm(it):
        def body(i, carry):
            rows = pl.ds(pl.multiple_of(32 * i, 32), 32)
            step = lax.div(i, 4)
            means = [stat[q, 0, rows] for q in range(4)]
            mean = (means[0] + means[1] + means[2] + means[3]) * 0.25
            square = jnp.zeros((32, 128), F32)
            for q in range(4):
                off = means[q] - mean
                square += stat[q, 1, rows] + QUART * off * off
            inv = lax.rsqrt(square / WIDTH + 1e-6)
            for q in range(4):
                for c in range(5):
                    cols = pl.ds(256 * c, 256)
                    m2 = jnp.concatenate([mean, mean], axis=1)
                    i2 = jnp.concatenate([inv, inv], axis=1)
                    d = (cur[it, q, rows, cols].astype(F32) - m2) * i2
                    shift = mods[q, pl.ds(step, 1), cols]
                    scale = mods[4 + q, pl.ds(step, 1), cols]
                    y[q, rows, cols] = (d * (1.0 + scale) + shift).astype(BF16)
            return carry

        lax.fori_loop(0, 8, body, 0)

    def project(k):
        def body(q, carry):
            rows = pl.ds(pl.multiple_of(q * QUART, 128), QUART)
            new = jnp.dot(y[q], w[k, rows], preferred_element_type=F32)
            acc[0] += new[:ROWS]
            uv[k, q] = new[ROWS:]
            return carry

        acc[0] = jnp.zeros((ROWS, HW), F32)
        lax.fori_loop(0, 4, body, 0)
        qkv[k] = acc[0].astype(BF16)

    def attention_block(it, c):
        for step in range(2):
            for n, h in enumerate(block_heads[c]):
                rows, cols = pl.ds(TOK * step, TOK), pl.ds(HEAD_SIZE * h, HEAD_SIZE)
                s = lax.dot_general(
                    qkv[0, rows, cols], qkv[1, rows, cols], (((1,), (1,)), ((), ())),
                    preferred_element_type=F32,
                ) * (1.0 / math.sqrt(HEAD_SIZE))
                e = jnp.exp(s - jnp.max(s, axis=-1, keepdims=True))
                p = (e / jnp.sum(e, axis=-1, keepdims=True)).astype(BF16)
                hd[c][it, x, rows, HEAD_SIZE * n : HEAD_SIZE * (n + 1)] = jnp.dot(
                    p, qkv[2, rows, cols], preferred_element_type=F32
                ).astype(BF16)
        hd_g[it][c].start(0, 3, 1, 2)

    def attention(it):
        for c in range(2):
            attention_block(it, c)

    def out_part(it, q, add):
        def body(i, carry):
            rows = pl.ds(pl.multiple_of(q * QUART + i * 256, 128), 256)
            cols = pl.ds(pl.multiple_of(i * 256, 128), 256)
            new = None
            for c in range(2):
                term = lax.dot_general(
                    hd[c][it, q], w[3, rows, blocks[c]], (((1,), (1,)), ((), ())),
                    preferred_element_type=F32,
                )
                new = term if new is None else new + term
            t[:, cols] = t[:, cols] + new if add else new
            return carry

        lax.fori_loop(0, 5, body, 0)

    def out_project(it):
        out_part(it, x, False)
        for g in hd_g[it]:
            g.recv(2)
        out_part(it, x3, True)
        for g in hd_g[it]:
            g.recv(3)
        out_part(it, x1, True)
        for g in hd_g[it]:
            g.recv(4, 5)
        out_part(it, x2, True)

    def hd_sent(it):
        for g in hd_g[it]:
            g.sent()

    first = jnp.where(tm == 0, 1.0, 0.0).astype(F32)

    def terms(it):
        def body(i, carry):
            rows = pl.ds(pl.multiple_of(16 * i, 16), 16)
            step = lax.div(i, 8)
            gate = mods[8, pl.ds(step, 1)] * hg_ref[step]
            t[rows] = gate * t[rows] + hg_ref[2 + step] * nz[rows].astype(F32)
            return carry

        lax.fori_loop(0, 16, body, 0)

        def body2(i, carry):
            rows = pl.ds(pl.multiple_of(16 * i, 16), 16)
            rows1 = pl.ds(pl.multiple_of(TOK + 16 * i, 16), 16)
            t0 = t[rows]
            tf[rows] = t0 + t[rows1] + first * cur[0, x, rows].astype(F32)
            if it == 0:
                tb[x, rows] = t0.astype(BF16)
            return carry

        lax.fori_loop(0, 8, body2, 0)

    mine = pl.ds(pl.multiple_of(64 * core, 64), 64)
    other = pl.ds(pl.multiple_of(64 - 64 * core, 64), 64)
    on0 = jnp.where(is0, 1.0, 0.0).astype(F32)
    on1 = 1.0 - on0

    def px_msg(it, m):
        if m == 0:
            src, dst, to = px_s, px_r.at[it], sib
        elif m == 1:
            src, dst, to = pe_s, pe_r.at[it], sib
        else:
            src, dst, to = sl_s, sl_r, before
        return remote(src, dst, px_ss.at[it, m], px_rs.at[it, m], to)

    starts = (0, 384, 768, 896)

    def piece_msg(it, way, d):
        h = lax.rem(chip + d, 16)
        src, dst = ((p1_s, p1_r), (p2_s, p2_r))[way]
        return remote(
            src.at[h], dst.at[it, chip], a_ss.at[it, way, d], a_rs.at[it, way, d],
            (2 * h + core, x),
        )

    def each(f):
        def body(d, carry):
            f(d)
            return carry

        lax.fori_loop(1, 16, body, 0)

    def prefix(it):
        px_s[...] = tf[other].astype(BF16)
        px_msg(it, 0).start()
        if it == ITERS - 1:
            sl_s[...] = t[0:TOK].astype(BF16)
            px_msg(it, 2).start()
        px_msg(it, 0).wait_recv()

        def loop(f):
            def body(i, carry):
                f(i, pl.ds(pl.multiple_of(16 * i, 16), 16),
                  pl.ds(pl.multiple_of(64 * core + 16 * i, 16), 16))
                return carry

            lax.fori_loop(0, 4, body, 0)

        def one(i, r, m):
            v = (tf[m] + px_r[it, r].astype(F32)).astype(BF16)
            for n, at in enumerate(starts):
                p1_s[4 * i + n] = v[:, at : at + 384]

        loop(one)
        each(lambda d: piece_msg(it, 0, d).start())
        p1_r[it, chip] = p1_s[chip]
        if it == 0:
            t0_g.forward()
        each(lambda d: piece_msg(it, 0, d).wait_recv())
        p = jnp.zeros((16, 384), F32)
        for g in range(16):
            p2_s[g] = p.astype(BF16)
            p += p1_r[it, g].astype(F32)
        each(lambda d: piece_msg(it, 1, d).start())
        p2_r[it, chip] = p2_s[chip]
        each(lambda d: piece_msg(it, 1, d).wait_recv())

        def three(i, r, m):
            cut = [p2_r[it, 4 * i + n].astype(F32) for n in range(4)]
            p = jnp.concatenate(cut[:3] + [cut[3][:, 256:]], axis=1)
            pe_s[r] = (p + on0 * tf[m]).astype(BF16)
            p += on1 * px_r[it, r].astype(F32) + first * cur[0, x, m].astype(F32)
            pfx[m] = p
            if it == 0:
                cur[1, x, m] = p.astype(BF16)

        loop(three)
        px_msg(it, 1).start()
        if it == 0:
            pfx_g.start(0, 3)
        px_msg(it, 1).wait_recv()

        def four(i, r, m):
            there = pl.ds(pl.multiple_of(64 - 64 * core + r.start, 16), 16)
            p = pe_r[it, r].astype(F32) + first * cur[0, x, there].astype(F32)
            pfx[there] = p
            if it == 0:
                cur[1, x, there] = p.astype(BF16)

        loop(four)
        if it == 0:
            pfx_g.start(2, 1)
        for m in range(2 + (it == ITERS - 1)):
            px_msg(it, m).wait_send()
        each(lambda d: piece_msg(it, 0, d).wait_send())
        each(lambda d: piece_msg(it, 1, d).wait_send())

    def slide():
        px_msg(ITERS - 1, 2).wait_recv()
        last = tm == 31

        def body(i, carry):
            rows = pl.ds(pl.multiple_of(16 * i, 16), 16)
            rows1 = pl.ds(pl.multiple_of(TOK + 16 * i, 16), 16)
            rows2 = pl.ds(pl.multiple_of(2 * TOK + 16 * i, 16), 16)
            c1 = pfx[rows] + t[rows]
            c2 = c1 + t[rows1]
            c3 = c2 + sl_r[rows].astype(F32)
            c2 = jnp.where(last, c1, c2)
            c3 = jnp.where(last, c1, c3)
            out_ref[rows] = c1.astype(BF16)
            out_ref[rows1] = c2.astype(BF16)
            out_ref[rows2] = c3.astype(BF16)
            return carry

        lax.fori_loop(0, 8, body, 0)

    swap_start()
    lat_g.start(0, 1, 2, 3)
    s0(0)
    s0(1)
    s1(0)
    s2(0)
    s0(2)
    s1(1)
    s2(1)
    lat_g.forward()
    s3(0)
    s1(2)
    s2(2)
    modulation()
    s3(1)
    s5(0)
    swap_finish()
    s0(3)
    block_stats(0, x)
    lat_g.recv(2, 3)
    block_stats(0, x1)
    block_stats(0, x3)
    lat_g.recv(4, 5)
    block_stats(0, x2)
    norm(0)
    s6(0)
    project(0)
    s3(2)
    s5(1)
    s1(3)
    s2(3)
    s6(1)
    project(1)
    s3(3, (0,))
    s5(2)
    s3(3, (1, 2))
    s6(2)
    project(2)
    attention(0)
    s3(3, (3,))
    for g in hd_g[0]:
        g.forward()
    s5(3)
    s6(3)
    out_project(0)
    terms(0)
    t0_g.start(0, 1, 2, 3)
    prefix(0)
    prepare(x)
    pfx_g.forward()
    block_project(x, whole, True)
    t0_g.recv(2, 3, 4, 5)
    pfx_g.recv(2)
    prepare(x3)
    block_project(x3, whole)
    pfx_g.recv(3)
    prepare(x1)
    block_project(x1, whole)
    pfx_g.recv(4, 5)
    prepare(x2)
    block_project(x2, blocks[0])
    finalize(0)
    attention_block(1, 0)
    block_project(x2, blocks[1])
    hd_g[1][0].forward()
    finalize(1)
    attention_block(1, 1)
    hd_g[1][1].forward()
    out_project(1)
    terms(1)
    prefix(1)
    slide()
    lax.fori_loop(0, 4, lambda k, c: (w_sent(k), c)[1], 0)
    lat_g.sent()
    t0_g.sent()
    pfx_g.sent()
    hd_sent(0)
    hd_sent(1)


def features(step_index, mod_table):
    half = mod_table.shape[0] // 2
    freqs = jnp.exp(-math.log(10000.0) * jnp.arange(half).astype(F32) / half)
    angles = step_index.astype(F32)[:, None] * freqs[None, :]
    return jnp.concatenate([jnp.cos(angles), jnp.sin(angles)], axis=1).astype(BF16)


def per_device(latents, noise, mod_table, w_query, w_key, w_value, w_out, step_index, slide_offset):
    feats = features(step_index, mod_table)
    feats = jnp.concatenate([feats, feats, jnp.zeros((12, feats.shape[1]), BF16)], axis=0)
    step_size = (step_index.astype(F32) + 1.0) / 2000.0
    hg = jnp.concatenate([step_size, 0.2 * jnp.sqrt(step_size)])
    hbm = pl.BlockSpec(memory_space=pl.ANY)
    vmem = pl.BlockSpec(memory_space=pltpu.VMEM)
    smem = pl.BlockSpec(memory_space=pltpu.SMEM)
    dma = pltpu.SemaphoreType.DMA
    out = pl.pallas_call(
        kernel,
        out_shape=jax.ShapeDtypeStruct((3 * TOK, QUART), BF16),
        in_specs=[hbm] * 7 + [vmem, smem],
        out_specs=vmem,
        scratch_shapes=[
            pltpu.VMEM((4, WIDTH, HW), BF16),
            pltpu.VMEM((ITERS, 4, ROWS, QUART), BF16),
            pltpu.VMEM((4, ROWS + 16, QUART), BF16),
            pltpu.VMEM((3, ROWS, HW), F32),
            pltpu.VMEM((3, 4, 16, HW), F32),
            pltpu.VMEM((3, ROWS, HW), BF16),
            pltpu.VMEM((ITERS, 4, ROWS, 256), BF16),
            pltpu.VMEM((ITERS, 4, ROWS, 384), BF16),
            pltpu.VMEM((4, ROWS, QUART), BF16),
            pltpu.VMEM((4, TOK, QUART), BF16),
            pltpu.VMEM((ROWS, QUART), F32),
            pltpu.VMEM((ROWS, QUART), BF16),
            pltpu.VMEM((9, 16, QUART), F32),
            pltpu.VMEM((4, 2, ROWS, 128), F32),
            pltpu.VMEM((TOK, QUART), F32),
            pltpu.VMEM((64, QUART), BF16),
            pltpu.VMEM((ITERS, 64, QUART), BF16),
            pltpu.VMEM((16, 16, 384), BF16),
            pltpu.VMEM((ITERS, 16, 16, 384), BF16),
            pltpu.VMEM((16, 16, 384), BF16),
            pltpu.VMEM((ITERS, 16, 16, 384), BF16),
            pltpu.VMEM((64, QUART), BF16),
            pltpu.VMEM((ITERS, 64, QUART), BF16),
            pltpu.VMEM((TOK, QUART), F32),
            pltpu.VMEM((TOK, QUART), BF16),
            pltpu.VMEM((TOK, QUART), BF16),
            dma((7,)),
            dma((4, N_MSG)),
            dma((4, N_MSG)),
            dma((3, 6)),
            dma((3, 6)),
            dma((ITERS, 2, 6)),
            dma((ITERS, 2, 6)),
            dma((ITERS, 3)),
            dma((ITERS, 3)),
            dma((ITERS, 2, 16)),
            dma((ITERS, 2, 16)),
            dma,
            dma,
        ],
        compiler_params=pltpu.CompilerParams(
            collective_id=0, has_side_effects=True, vmem_limit_bytes=62 * 1024 * 1024
        ),
        cost_estimate=pl.CostEstimate(
            flops=2 * ITERS * 4 * ROWS * WIDTH * HW, bytes_accessed=12_000_000, transcendentals=0
        ),
    )(
        latents.reshape(ROWS, QUART), noise.reshape(ROWS, QUART), mod_table,
        w_query, w_key, w_value, w_out.T, feats, hg,
    )
    return lax.dynamic_slice_in_dim(out.reshape(3, TOK, QUART), slide_offset - 1, 2, 0)


def solution(mesh):
    placed = (
        P("tm", None, "tp"),
        P("tm", None, "tp"),
        P(),
        P("tm", "tp"),
        P("tm", "tp"),
        P("tm", "tp"),
        P("tp", "tm"),
        P("tm"),
        P(),
    )
    return jax.shard_map(
        per_device, mesh=mesh, in_specs=placed, out_specs=P("tm", None, "tp"), check_vma=False
    )
```

```python
import functools
import math

import jax
import jax.numpy as jnp
from jax import lax
from jax.experimental import pallas as pl
from jax.experimental.pallas import tpu as pltpu
from jax.sharding import PartitionSpec as P

HEAD_SIZE = 128
HEADS = 5
ITERS = 2
TOK = 128
ROWS = 256
QUART = 1280
WIDTH = 5120
HW = 640
SHARD = 160
HALF = 80
MESH = pl.DeviceIdType.MESH
F32 = jnp.float32
BF16 = jnp.bfloat16
N_MSG = 36


def kernel(
    lat_ref, noise_ref, table_ref, wq_ref, wk_ref, wv_ref, wo_ref, feats_ref, hg_ref,
    out_ref,
    w, cur, y, acc, uv, qkv, hda, hdb, part, tb, t, nz, mods, stat,
    tf, px_s, px_r, p1_s, p1_r, p2_s, p2_r, pe_s, pe_r, pfx, sl_s, sl_r,
    loc_sem, w_ss, w_rs, ag_ss, ag_rs, hd_ss, hd_rs, px_ss, px_rs, a_ss, a_rs, tr_ss, tr_rs,
):
    tm = lax.axis_index("tm")
    x = lax.axis_index("tp")
    core = lax.rem(tm, 2)
    chip = lax.div(tm, 2)
    yy, zz = lax.div(chip, 4), lax.rem(chip, 4)
    is0 = core == 0
    a = jnp.where(is0, zz, yy)
    b = jnp.where(is0, yy, zz)

    def rank(da, db):
        aa, bb = lax.rem(a + da, 4), lax.rem(b + db, 4)
        return jnp.where(is0, bb * 4 + aa, aa * 4 + bb) * 2 + core

    def dev(da, db):
        return (rank(da, db), x)

    sib = (tm + 1 - 2 * core, x)
    xp = (tm, lax.rem(x + 1, 4))
    xm = (tm, lax.rem(x + 3, 4))
    following = (lax.rem(tm + 1, 32), x)
    before = (lax.rem(tm + 31, 32), x)
    swapped = ((x * 4 + zz) * 2 + core, yy)
    swaps = x != yy
    x1, x2, x3 = lax.rem(x + 1, 4), lax.rem(x + 2, 4), lax.rem(x + 3, 4)

    def remote(src, dst, ss, rs, to):
        return pltpu.make_async_remote_copy(
            src_ref=src, dst_ref=dst, send_sem=ss, recv_sem=rs, device_id=to, device_id_type=MESH
        )

    own = pl.ds(pl.multiple_of(SHARD * tm, 16), SHARD)
    local = [
        pltpu.make_async_copy(src, w.at[k, own], loc_sem.at[k])
        for k, src in enumerate((wq_ref, wk_ref, wv_ref))
    ]
    local.append(pltpu.make_async_copy(lat_ref, cur.at[0, x], loc_sem.at[4]))
    local.append(pltpu.make_async_copy(noise_ref, nz, loc_sem.at[5]))
    for c in local:
        c.start()

    barrier = pltpu.get_barrier_semaphore()
    peers = [sib, xp, xm, following, before]
    peers += [(2 * lax.rem(chip + d, 16) + core, x) for d in range(1, 16)]
    for peer in peers:
        pl.semaphore_signal(barrier, inc=1, device_id=peer, device_id_type=MESH)

    @pl.when(swaps)
    def _():
        pl.semaphore_signal(barrier, inc=1, device_id=swapped, device_id_type=MESH)

    pl.semaphore_wait(barrier, len(peers) + jnp.where(swaps, 1, 0))

    def swap_msg():
        there = pl.ds(pl.multiple_of(SHARD * swapped[0], 16), SHARD)
        return remote(wo_ref, w.at[3, there], tr_ss, tr_rs, swapped)

    def swap_local():
        return pltpu.make_async_copy(wo_ref, w.at[3, own], loc_sem.at[6])

    def swap_start():
        @pl.when(swaps)
        def _():
            swap_msg().start()

        @pl.when(jnp.logical_not(swaps))
        def _():
            swap_local().start()

    def swap_finish():
        @pl.when(swaps)
        def _():
            swap_msg().wait()

        @pl.when(jnp.logical_not(swaps))
        def _():
            swap_local().wait()

    for c in local:
        c.wait()

    class Gather:
        def __init__(self, block, halves, ss, rs):
            self.block, self.halves, self.ss, self.rs = block, halves, ss, rs

        def msg(self, m):
            to = xp if m in (0, 2, 4) else xm
            src = (x, x, x, x, x3, x1)[m]
            ref = self.block(src, self.halves[(0, 1, 1, 0, 0, 1)[m]])
            return remote(ref, ref, self.ss(m), self.rs(m), to)

        def start(self, *ms):
            for m in ms:
                self.msg(m).start()

        def forward(self):
            self.msg(0).wait_recv()
            self.msg(4).start()
            self.msg(1).wait_recv()
            self.msg(5).start()

        def recv(self, *ms):
            for m in ms:
                self.msg(m).wait_recv()

        def sent(self):
            for m in range(6):
                self.msg(m).wait_send()

    steps = (pl.ds(0, TOK), pl.ds(TOK, TOK))
    lat_g = Gather(lambda q, r: cur.at[0, q, r], steps, lambda m: ag_ss.at[0, m], lambda m: ag_rs.at[0, m])
    t0_g = Gather(
        lambda q, r: tb.at[q, r], (pl.ds(0, 64), pl.ds(64, 64)),
        lambda m: ag_ss.at[1, m], lambda m: ag_rs.at[1, m],
    )
    pfx_g = Gather(
        lambda q, r: cur.at[1, q, r],
        (pl.ds(pl.multiple_of(64 * core, 64), 64), pl.ds(pl.multiple_of(64 - 64 * core, 64), 64)),
        lambda m: ag_ss.at[2, m], lambda m: ag_rs.at[2, m],
    )
    hd = (hda, hdb)
    blocks = (pl.ds(0, 256), pl.ds(256, 384))
    block_heads = ((0, 1), (2, 3, 4))
    whole = pl.ds(0, HW)

    def hd_gather(it, c):
        return Gather(
            lambda q, r: hd[c].at[it, q, r], steps,
            lambda m: hd_ss.at[it, c, m], lambda m: hd_rs.at[it, c, m],
        )

    hd_g = [[hd_gather(it, c) for c in range(2)] for it in range(ITERS)]

    def rows_of(r, lo, n):
        return pl.ds(pl.multiple_of(SHARD * r + lo, 16), n)

    def w_msg(k, m):
        if m < 4:
            ref = (
                w.at[k, rows_of(tm, 0, SHARD)],
                w.at[k, rows_of(tm, 0, SHARD)],
                w.at[k, rows_of(rank(3, 0), 0, HALF)],
                w.at[k, rows_of(rank(1, 0), HALF, HALF)],
            )[m]
            to = dev(1, 0) if m in (0, 2) else dev(3, 0)
        elif m < 20:
            j, i = divmod(m - 4, 4)
            da = (0, 3, 1, 2)[j]
            ref = (
                w.at[k, rows_of(rank(da, 0), 0, SHARD)],
                w.at[k, rows_of(rank(da, 0), 0, SHARD)],
                w.at[k, rows_of(rank(da, 3), 0, HALF)],
                w.at[k, rows_of(rank(da, 1), HALF, HALF)],
            )[i]
            to = dev(0, 1) if i in (0, 2) else dev(0, 3)
        else:
            j, i = divmod(m - 20, 4)
            ref = w.at[k, rows_of(rank((0, 3, 1, 2)[j], (0, 3, 1, 2)[i]), 0, SHARD)]
            to = sib
        return remote(ref, ref, w_ss.at[k, m], w_rs.at[k, m], to)

    def w_start(k, *ms):
        for m in ms:
            w_msg(k, m).start()

    def w_recv(k, *ms):
        for m in ms:
            w_msg(k, m).wait_recv()

    def s0(k):
        w_start(k, 0, 1, 4, 5, 20)

    def s1(k):
        w_recv(k, 0)
        w_start(k, 2, 8, 9, 24)
        w_recv(k, 1)
        w_start(k, 3, 12, 13, 28)

    def s2(k):
        w_recv(k, 2, 3)
        w_start(k, 16, 17, 32)

    def s3(k, parts=(0, 1, 2, 3)):
        for j in parts:
            w_recv(k, 4 + 4 * j)
            w_start(k, 6 + 4 * j, 21 + 4 * j)
            w_recv(k, 5 + 4 * j)
            w_start(k, 7 + 4 * j, 22 + 4 * j)

    def s5(k):
        for j in range(4):
            w_recv(k, 6 + 4 * j, 7 + 4 * j)
            w_start(k, 23 + 4 * j)

    def s6(k):
        for m in range(20, 36):
            w_msg(k, m).wait_recv()

    def w_sent(k):
        for m in range(N_MSG):
            w_msg(k, m).wait_send()

    def modulation():
        for base in (0, 4, 8):
            count = 4 if base < 8 else 1
            for k in range(count):
                start = (base + k) * QUART if base < 8 else 2 * WIDTH + x * QUART
                pltpu.make_async_copy(
                    table_ref.at[:, pl.ds(pl.multiple_of(start, 128), QUART)],
                    part.at[k], loc_sem.at[k],
                ).start()
            for k in range(count):
                pltpu.make_async_copy(
                    table_ref.at[:, pl.ds(0, QUART)], part.at[k], loc_sem.at[k]
                ).wait()
                mods[base + k] = jnp.dot(feats_ref[...], part[k], preferred_element_type=F32)
        row = lax.broadcasted_iota(jnp.int32, (16, QUART), 0)
        for q in range(4):
            rows = jnp.where(row < 2, 1.0 + mods[4 + q], jnp.where(row < 4, mods[q], 0.0))
            y[q, ROWS : ROWS + 16] = rows.astype(BF16)

    def block_stats(it, q):
        def body(i, carry):
            rows = pl.ds(pl.multiple_of(32 * i, 32), 32)
            c = cur[it, q, rows].astype(F32)
            mean = jnp.sum(c, axis=-1, keepdims=True) / QUART
            d = c - mean
            stat[q, 0, rows] = jnp.broadcast_to(mean, (32, 128))
            stat[q, 1, rows] = jnp.broadcast_to(jnp.sum(d * d, axis=-1, keepdims=True), (32, 128))
            return carry

        lax.fori_loop(0, 8, body, 0)

    def prepare(q):
        def body(i, carry):
            rows = pl.ds(pl.multiple_of(32 * i, 32), 32)
            p = cur[1, q, rows].astype(F32)
            for step in range(2):
                here = pl.ds(pl.multiple_of(TOK * step + 32 * i, 32), 32)
                c = p if step == 0 else p + tb[q, rows].astype(F32)
                mean = jnp.sum(c, axis=-1, keepdims=True) / QUART
                d = c - mean
                stat[q, 0, here] = jnp.broadcast_to(mean, (32, 128))
                stat[q, 1, here] = jnp.broadcast_to(
                    jnp.sum(d * d, axis=-1, keepdims=True), (32, 128)
                )
                y[q, here] = (d * (1.0 + mods[4 + q, step : step + 1])).astype(BF16)
            return carry

        lax.fori_loop(0, 4, body, 0)

    def block_project(q, cols, first=False):
        rows = pl.ds(pl.multiple_of(q * QUART, 128), QUART)

        def body(k, carry):
            new = jnp.dot(y[q, 0:ROWS], w[k, rows, cols], preferred_element_type=F32)
            acc[k, :, cols] = new if first else acc[k, :, cols] + new
            return carry

        lax.fori_loop(0, 3, body, 0)

    def finalize(c):
        def body(step, i, carry):
            rows = pl.ds(pl.multiple_of(TOK * step + 32 * i, 32), 32)
            means = [stat[q, 0, rows] for q in range(4)]
            mean = (means[0] + means[1] + means[2] + means[3]) * 0.25
            offs = [m - mean for m in means]
            square = jnp.zeros((32, 128), F32)
            for q in range(4):
                square += stat[q, 1, rows] + QUART * offs[q] * offs[q]
            inv = lax.rsqrt(square / WIDTH + 1e-6)
            for k in range(3):
                for h in block_heads[c]:
                    cols = pl.ds(HEAD_SIZE * h, HEAD_SIZE)
                    value = acc[k, rows, cols]
                    add = jnp.zeros((1, HEAD_SIZE), F32)
                    for q in range(4):
                        value += offs[q] * uv[k, q, step : step + 1, cols]
                        add += uv[k, q, 2 + step : 3 + step, cols]
                    qkv[k, rows, cols] = (inv * value + add).astype(BF16)
            return carry

        for step in range(2):
            lax.fori_loop(0, 4, functools.partial(body, step), 0)

    def norm(it):
        def body(i, carry):
            rows = pl.ds(pl.multiple_of(32 * i, 32), 32)
            step = lax.div(i, 4)
            means = [stat[q, 0, rows] for q in range(4)]
            mean = (means[0] + means[1] + means[2] + means[3]) * 0.25
            square = jnp.zeros((32, 128), F32)
            for q in range(4):
                off = means[q] - mean
                square += stat[q, 1, rows] + QUART * off * off
            inv = lax.rsqrt(square / WIDTH + 1e-6)
            for q in range(4):
                for c in range(5):
                    cols = pl.ds(256 * c, 256)
                    m2 = jnp.concatenate([mean, mean], axis=1)
                    i2 = jnp.concatenate([inv, inv], axis=1)
                    d = (cur[it, q, rows, cols].astype(F32) - m2) * i2
                    shift = mods[q, pl.ds(step, 1), cols]
                    scale = mods[4 + q, pl.ds(step, 1), cols]
                    y[q, rows, cols] = (d * (1.0 + scale) + shift).astype(BF16)
            return carry

        lax.fori_loop(0, 8, body, 0)

    def project(k, cols):
        def body(q, carry):
            rows = pl.ds(pl.multiple_of(q * QUART, 128), QUART)
            new = jnp.dot(y[q], w[k, rows, cols], preferred_element_type=F32)
            acc[0, :, cols] += new[:ROWS]
            uv[k, q, :, cols] = new[ROWS:]
            return carry

        acc[0, :, cols] = jnp.zeros((ROWS, cols.size), F32)
        lax.fori_loop(0, 4, body, 0)
        qkv[k, :, cols] = acc[0, :, cols].astype(BF16)

    def attention_block(it, c):
        for step in range(2):
            for n, h in enumerate(block_heads[c]):
                rows, cols = pl.ds(TOK * step, TOK), pl.ds(HEAD_SIZE * h, HEAD_SIZE)
                s = lax.dot_general(
                    qkv[0, rows, cols], qkv[1, rows, cols], (((1,), (1,)), ((), ())),
                    preferred_element_type=F32,
                ) * (1.0 / math.sqrt(HEAD_SIZE))
                e = jnp.exp(s - jnp.max(s, axis=-1, keepdims=True))
                p = (e / jnp.sum(e, axis=-1, keepdims=True)).astype(BF16)
                hd[c][it, x, rows, HEAD_SIZE * n : HEAD_SIZE * (n + 1)] = jnp.dot(
                    p, qkv[2, rows, cols], preferred_element_type=F32
                ).astype(BF16)
        hd_g[it][c].start(0, 1, 2, 3)

    def out_part(it, q, add):
        def body(i, carry):
            rows = pl.ds(pl.multiple_of(q * QUART + i * 256, 128), 256)
            cols = pl.ds(pl.multiple_of(i * 256, 128), 256)
            new = None
            for c in range(2):
                term = lax.dot_general(
                    hd[c][it, q], w[3, rows, blocks[c]], (((1,), (1,)), ((), ())),
                    preferred_element_type=F32,
                )
                new = term if new is None else new + term
            t[:, cols] = t[:, cols] + new if add else new
            return carry

        lax.fori_loop(0, 5, body, 0)

    def out_project(it):
        out_part(it, x, False)
        for g in hd_g[it]:
            g.recv(2)
        out_part(it, x3, True)
        for g in hd_g[it]:
            g.recv(3)
        out_part(it, x1, True)
        for g in hd_g[it]:
            g.recv(4, 5)
        out_part(it, x2, True)

    def hd_sent(it):
        for g in hd_g[it]:
            g.sent()

    first = jnp.where(tm == 0, 1.0, 0.0).astype(F32)

    def terms(it):
        def body(i, carry):
            rows = pl.ds(pl.multiple_of(16 * i, 16), 16)
            step = lax.div(i, 8)
            gate = mods[8, pl.ds(step, 1)] * hg_ref[step]
            t[rows] = gate * t[rows] + hg_ref[2 + step] * nz[rows].astype(F32)
            return carry

        lax.fori_loop(0, 16, body, 0)

        def body2(i, carry):
            rows = pl.ds(pl.multiple_of(16 * i, 16), 16)
            rows1 = pl.ds(pl.multiple_of(TOK + 16 * i, 16), 16)
            t0 = t[rows]
            tf[rows] = t0 + t[rows1] + first * cur[0, x, rows].astype(F32)
            if it == 0:
                tb[x, rows] = t0.astype(BF16)
            return carry

        lax.fori_loop(0, 8, body2, 0)

    mine = pl.ds(pl.multiple_of(64 * core, 64), 64)
    other = pl.ds(pl.multiple_of(64 - 64 * core, 64), 64)
    on0 = jnp.where(is0, 1.0, 0.0).astype(F32)
    on1 = 1.0 - on0

    def px_msg(it, m):
        if m == 0:
            src, dst, to = px_s, px_r.at[it], sib
        elif m == 1:
            src, dst, to = pe_s, pe_r.at[it], sib
        else:
            src, dst, to = sl_s, sl_r, before
        return remote(src, dst, px_ss.at[it, m], px_rs.at[it, m], to)

    starts = (0, 384, 768, 896)

    def piece_msg(it, way, d):
        h = lax.rem(chip + d, 16)
        src, dst = ((p1_s, p1_r), (p2_s, p2_r))[way]
        return remote(
            src.at[h], dst.at[it, chip], a_ss.at[it, way, d], a_rs.at[it, way, d],
            (2 * h + core, x),
        )

    def each(f):
        def body(d, carry):
            f(d)
            return carry

        lax.fori_loop(1, 16, body, 0)

    def prefix(it):
        px_s[...] = tf[other].astype(BF16)
        px_msg(it, 0).start()
        if it == ITERS - 1:
            sl_s[...] = t[0:TOK].astype(BF16)
            px_msg(it, 2).start()
        px_msg(it, 0).wait_recv()

        def loop(f):
            def body(i, carry):
                f(i, pl.ds(pl.multiple_of(16 * i, 16), 16),
                  pl.ds(pl.multiple_of(64 * core + 16 * i, 16), 16))
                return carry

            lax.fori_loop(0, 4, body, 0)

        def one(i, r, m):
            v = (tf[m] + px_r[it, r].astype(F32)).astype(BF16)
            for n, at in enumerate(starts):
                p1_s[4 * i + n] = v[:, at : at + 384]

        loop(one)
        each(lambda d: piece_msg(it, 0, d).start())
        p1_r[it, chip] = p1_s[chip]
        if it == 0:
            t0_g.forward()
        each(lambda d: piece_msg(it, 0, d).wait_recv())
        p = jnp.zeros((16, 384), F32)
        for g in range(16):
            p2_s[g] = p.astype(BF16)
            p += p1_r[it, g].astype(F32)
        each(lambda d: piece_msg(it, 1, d).start())
        p2_r[it, chip] = p2_s[chip]
        each(lambda d: piece_msg(it, 1, d).wait_recv())

        def three(i, r, m):
            cut = [p2_r[it, 4 * i + n].astype(F32) for n in range(4)]
            p = jnp.concatenate(cut[:3] + [cut[3][:, 256:]], axis=1)
            pe_s[r] = (p + on0 * tf[m]).astype(BF16)
            p += on1 * px_r[it, r].astype(F32) + first * cur[0, x, m].astype(F32)
            pfx[m] = p
            if it == 0:
                cur[1, x, m] = p.astype(BF16)

        loop(three)
        px_msg(it, 1).start()
        if it == 0:
            pfx_g.start(0)
        px_msg(it, 1).wait_recv()

        def four(i, r, m):
            there = pl.ds(pl.multiple_of(64 - 64 * core + r.start, 16), 16)
            p = pe_r[it, r].astype(F32) + first * cur[0, x, there].astype(F32)
            pfx[there] = p
            if it == 0:
                cur[1, x, there] = p.astype(BF16)

        loop(four)
        if it == 0:
            pfx_g.start(1, 2, 3)
        for m in range(2 + (it == ITERS - 1)):
            px_msg(it, m).wait_send()
        each(lambda d: piece_msg(it, 0, d).wait_send())
        each(lambda d: piece_msg(it, 1, d).wait_send())

    def slide():
        px_msg(ITERS - 1, 2).wait_recv()
        last = tm == 31

        def body(i, carry):
            rows = pl.ds(pl.multiple_of(16 * i, 16), 16)
            rows1 = pl.ds(pl.multiple_of(TOK + 16 * i, 16), 16)
            rows2 = pl.ds(pl.multiple_of(2 * TOK + 16 * i, 16), 16)
            c1 = pfx[rows] + t[rows]
            c2 = c1 + t[rows1]
            c3 = c2 + sl_r[rows].astype(F32)
            c2 = jnp.where(last, c1, c2)
            c3 = jnp.where(last, c1, c3)
            out_ref[rows] = c1.astype(BF16)
            out_ref[rows1] = c2.astype(BF16)
            out_ref[rows2] = c3.astype(BF16)
            return carry

        lax.fori_loop(0, 8, body, 0)

    swap_start()
    lat_g.start(0, 1, 2, 3)
    s0(0)
    s0(1)
    s1(0)
    s2(0)
    s0(2)
    s1(1)
    s2(1)
    lat_g.forward()
    s3(0)
    s1(2)
    s2(2)
    modulation()
    s3(1)
    s5(0)
    swap_finish()
    s0(3)
    block_stats(0, x)
    lat_g.recv(2, 3)
    block_stats(0, x1)
    block_stats(0, x3)
    lat_g.recv(4, 5)
    block_stats(0, x2)
    norm(0)
    s6(0)
    project(0, whole)
    s3(2)
    s5(1)
    s1(3)
    s2(3)
    s6(1)
    project(1, whole)
    s3(3, (0,))
    s5(2)
    s3(3, (1, 2))
    s6(2)
    project(2, blocks[0])
    attention_block(0, 0)
    project(2, blocks[1])
    attention_block(0, 1)
    s3(3, (3,))
    for g in hd_g[0]:
        g.forward()
    s5(3)
    s6(3)
    out_project(0)
    terms(0)
    t0_g.start(0, 1, 2, 3)
    prefix(0)
    prepare(x)
    pfx_g.forward()
    block_project(x, whole, True)
    t0_g.recv(2, 3, 4, 5)
    pfx_g.recv(2)
    prepare(x3)
    block_project(x3, whole)
    pfx_g.recv(3)
    prepare(x1)
    block_project(x1, whole)
    pfx_g.recv(4, 5)
    prepare(x2)
    block_project(x2, blocks[0])
    finalize(0)
    attention_block(1, 0)
    block_project(x2, blocks[1])
    hd_g[1][0].forward()
    finalize(1)
    attention_block(1, 1)
    hd_g[1][1].forward()
    out_project(1)
    terms(1)
    prefix(1)
    slide()
    lax.fori_loop(0, 4, lambda k, c: (w_sent(k), c)[1], 0)
    lat_g.sent()
    t0_g.sent()
    pfx_g.sent()
    hd_sent(0)
    hd_sent(1)


def features(step_index, mod_table):
    half = mod_table.shape[0] // 2
    freqs = jnp.exp(-math.log(10000.0) * jnp.arange(half).astype(F32) / half)
    angles = step_index.astype(F32)[:, None] * freqs[None, :]
    return jnp.concatenate([jnp.cos(angles), jnp.sin(angles)], axis=1).astype(BF16)


def per_device(latents, noise, mod_table, w_query, w_key, w_value, w_out, step_index, slide_offset):
    feats = features(step_index, mod_table)
    feats = jnp.concatenate([feats, feats, jnp.zeros((12, feats.shape[1]), BF16)], axis=0)
    step_size = (step_index.astype(F32) + 1.0) / 2000.0
    hg = jnp.concatenate([step_size, 0.2 * jnp.sqrt(step_size)])
    hbm = pl.BlockSpec(memory_space=pl.ANY)
    vmem = pl.BlockSpec(memory_space=pltpu.VMEM)
    smem = pl.BlockSpec(memory_space=pltpu.SMEM)
    dma = pltpu.SemaphoreType.DMA
    out = pl.pallas_call(
        kernel,
        out_shape=jax.ShapeDtypeStruct((3 * TOK, QUART), BF16),
        in_specs=[hbm] * 7 + [vmem, smem],
        out_specs=vmem,
        scratch_shapes=[
            pltpu.VMEM((4, WIDTH, HW), BF16),
            pltpu.VMEM((ITERS, 4, ROWS, QUART), BF16),
            pltpu.VMEM((4, ROWS + 16, QUART), BF16),
            pltpu.VMEM((3, ROWS, HW), F32),
            pltpu.VMEM((3, 4, 16, HW), F32),
            pltpu.VMEM((3, ROWS, HW), BF16),
            pltpu.VMEM((ITERS, 4, ROWS, 256), BF16),
            pltpu.VMEM((ITERS, 4, ROWS, 384), BF16),
            pltpu.VMEM((4, ROWS, QUART), BF16),
            pltpu.VMEM((4, TOK, QUART), BF16),
            pltpu.VMEM((ROWS, QUART), F32),
            pltpu.VMEM((ROWS, QUART), BF16),
            pltpu.VMEM((9, 16, QUART), F32),
            pltpu.VMEM((4, 2, ROWS, 128), F32),
            pltpu.VMEM((TOK, QUART), F32),
            pltpu.VMEM((64, QUART), BF16),
            pltpu.VMEM((ITERS, 64, QUART), BF16),
            pltpu.VMEM((16, 16, 384), BF16),
            pltpu.VMEM((ITERS, 16, 16, 384), BF16),
            pltpu.VMEM((16, 16, 384), BF16),
            pltpu.VMEM((ITERS, 16, 16, 384), BF16),
            pltpu.VMEM((64, QUART), BF16),
            pltpu.VMEM((ITERS, 64, QUART), BF16),
            pltpu.VMEM((TOK, QUART), F32),
            pltpu.VMEM((TOK, QUART), BF16),
            pltpu.VMEM((TOK, QUART), BF16),
            dma((7,)),
            dma((4, N_MSG)),
            dma((4, N_MSG)),
            dma((3, 6)),
            dma((3, 6)),
            dma((ITERS, 2, 6)),
            dma((ITERS, 2, 6)),
            dma((ITERS, 3)),
            dma((ITERS, 3)),
            dma((ITERS, 2, 16)),
            dma((ITERS, 2, 16)),
            dma,
            dma,
        ],
        compiler_params=pltpu.CompilerParams(
            collective_id=0, has_side_effects=True, vmem_limit_bytes=62 * 1024 * 1024
        ),
        cost_estimate=pl.CostEstimate(
            flops=2 * ITERS * 4 * ROWS * WIDTH * HW, bytes_accessed=12_000_000, transcendentals=0
        ),
    )(
        latents.reshape(ROWS, QUART), noise.reshape(ROWS, QUART), mod_table,
        w_query, w_key, w_value, w_out.T, feats, hg,
    )
    return lax.dynamic_slice_in_dim(out.reshape(3, TOK, QUART), slide_offset - 1, 2, 0)


def solution(mesh):
    placed = (
        P("tm", None, "tp"),
        P("tm", None, "tp"),
        P(),
        P("tm", "tp"),
        P("tm", "tp"),
        P("tm", "tp"),
        P("tp", "tm"),
        P("tm"),
        P(),
    )
    return jax.shard_map(
        per_device, mesh=mesh, in_specs=placed, out_specs=P("tm", None, "tp"), check_vma=False
    )
```

```python
import functools
import math

import jax
import jax.numpy as jnp
from jax import lax
from jax.experimental import pallas as pl
from jax.experimental.pallas import tpu as pltpu
from jax.sharding import PartitionSpec as P

HEAD_SIZE = 128
HEADS = 5
ITERS = 2
TOK = 128
ROWS = 256
QUART = 1280
WIDTH = 5120
HW = 640
SHARD = 160
HALF = 80
MESH = pl.DeviceIdType.MESH
F32 = jnp.float32
BF16 = jnp.bfloat16
N_MSG = 36


def kernel(
    lat_ref, noise_ref, table_ref, wq_ref, wk_ref, wv_ref, wo_ref, feats_ref, index_ref,
    out_ref,
    w, cur, y, acc, uv, qkv, hda, hdb, part, tb, t, nz, mods, stat,
    tf, px_s, px_r, p1_s, p1_r, p2_s, p2_r, pe_s, pe_r, pfx, sl_s, sl_r,
    loc_sem, w_ss, w_rs, ag_ss, ag_rs, hd_ss, hd_rs, px_ss, px_rs, a_ss, a_rs, tr_ss, tr_rs,
):
    tm = lax.axis_index("tm")
    x = lax.axis_index("tp")
    core = lax.rem(tm, 2)
    chip = lax.div(tm, 2)
    yy, zz = lax.div(chip, 4), lax.rem(chip, 4)
    is0 = core == 0
    a = jnp.where(is0, zz, yy)
    b = jnp.where(is0, yy, zz)

    def rank(da, db):
        aa, bb = lax.rem(a + da, 4), lax.rem(b + db, 4)
        return jnp.where(is0, bb * 4 + aa, aa * 4 + bb) * 2 + core

    def dev(da, db):
        return (rank(da, db), x)

    sib = (tm + 1 - 2 * core, x)
    xp = (tm, lax.rem(x + 1, 4))
    xm = (tm, lax.rem(x + 3, 4))
    following = (lax.rem(tm + 1, 32), x)
    before = (lax.rem(tm + 31, 32), x)
    swapped = ((x * 4 + zz) * 2 + core, yy)
    swaps = x != yy
    x1, x2, x3 = lax.rem(x + 1, 4), lax.rem(x + 2, 4), lax.rem(x + 3, 4)

    def remote(src, dst, ss, rs, to):
        return pltpu.make_async_remote_copy(
            src_ref=src, dst_ref=dst, send_sem=ss, recv_sem=rs, device_id=to, device_id_type=MESH
        )

    own = pl.ds(pl.multiple_of(SHARD * tm, 16), SHARD)
    local = [
        pltpu.make_async_copy(src, w.at[k, own], loc_sem.at[k])
        for k, src in enumerate((wq_ref, wk_ref, wv_ref))
    ]
    local.append(pltpu.make_async_copy(lat_ref, cur.at[0, x], loc_sem.at[4]))
    local.append(pltpu.make_async_copy(noise_ref, nz, loc_sem.at[5]))
    for c in local:
        c.start()

    barrier = pltpu.get_barrier_semaphore()
    peers = [sib, xp, xm, following, before]
    peers += [(2 * lax.rem(chip + d, 16) + core, x) for d in range(1, 16)]
    for peer in peers:
        pl.semaphore_signal(barrier, inc=1, device_id=peer, device_id_type=MESH)

    @pl.when(swaps)
    def _():
        pl.semaphore_signal(barrier, inc=1, device_id=swapped, device_id_type=MESH)

    pl.semaphore_wait(barrier, len(peers) + jnp.where(swaps, 1, 0))

    def swap_msg():
        there = pl.ds(pl.multiple_of(SHARD * swapped[0], 16), SHARD)
        return remote(wo_ref, w.at[3, there], tr_ss, tr_rs, swapped)

    def swap_local():
        return pltpu.make_async_copy(wo_ref, w.at[3, own], loc_sem.at[6])

    def swap_start():
        @pl.when(swaps)
        def _():
            swap_msg().start()

        @pl.when(jnp.logical_not(swaps))
        def _():
            swap_local().start()

    def swap_finish():
        @pl.when(swaps)
        def _():
            swap_msg().wait()

        @pl.when(jnp.logical_not(swaps))
        def _():
            swap_local().wait()

    for c in local:
        c.wait()

    class Gather:
        def __init__(self, block, halves, ss, rs):
            self.block, self.halves, self.ss, self.rs = block, halves, ss, rs

        def msg(self, m):
            to = xp if m in (0, 2, 4) else xm
            src = (x, x, x, x, x3, x1)[m]
            ref = self.block(src, self.halves[(0, 1, 1, 0, 0, 1)[m]])
            return remote(ref, ref, self.ss(m), self.rs(m), to)

        def start(self, *ms):
            for m in ms:
                self.msg(m).start()

        def forward(self):
            self.msg(0).wait_recv()
            self.msg(4).start()
            self.msg(1).wait_recv()
            self.msg(5).start()

        def recv(self, *ms):
            for m in ms:
                self.msg(m).wait_recv()

        def sent(self):
            for m in range(6):
                self.msg(m).wait_send()

    steps = (pl.ds(0, TOK), pl.ds(TOK, TOK))
    lat_g = Gather(lambda q, r: cur.at[0, q, r], steps, lambda m: ag_ss.at[0, m], lambda m: ag_rs.at[0, m])
    t0_g = Gather(
        lambda q, r: tb.at[q, r], (pl.ds(0, 64), pl.ds(64, 64)),
        lambda m: ag_ss.at[1, m], lambda m: ag_rs.at[1, m],
    )
    pfx_g = Gather(
        lambda q, r: cur.at[1, q, r],
        (pl.ds(pl.multiple_of(64 * core, 64), 64), pl.ds(pl.multiple_of(64 - 64 * core, 64), 64)),
        lambda m: ag_ss.at[2, m], lambda m: ag_rs.at[2, m],
    )
    hd = (hda, hdb)
    blocks = (pl.ds(0, 256), pl.ds(256, 384))
    block_heads = ((0, 1), (2, 3, 4))
    whole = pl.ds(0, HW)

    def hd_gather(it, c):
        return Gather(
            lambda q, r: hd[c].at[it, q, r], steps,
            lambda m: hd_ss.at[it, c, m], lambda m: hd_rs.at[it, c, m],
        )

    hd_g = [[hd_gather(it, c) for c in range(2)] for it in range(ITERS)]

    def rows_of(r, lo, n):
        return pl.ds(pl.multiple_of(SHARD * r + lo, 16), n)

    def w_msg(k, m):
        if m < 4:
            ref = (
                w.at[k, rows_of(tm, 0, SHARD)],
                w.at[k, rows_of(tm, 0, SHARD)],
                w.at[k, rows_of(rank(3, 0), 0, HALF)],
                w.at[k, rows_of(rank(1, 0), HALF, HALF)],
            )[m]
            to = dev(1, 0) if m in (0, 2) else dev(3, 0)
        elif m < 20:
            j, i = divmod(m - 4, 4)
            da = (0, 3, 1, 2)[j]
            ref = (
                w.at[k, rows_of(rank(da, 0), 0, SHARD)],
                w.at[k, rows_of(rank(da, 0), 0, SHARD)],
                w.at[k, rows_of(rank(da, 3), 0, HALF)],
                w.at[k, rows_of(rank(da, 1), HALF, HALF)],
            )[i]
            to = dev(0, 1) if i in (0, 2) else dev(0, 3)
        else:
            j, i = divmod(m - 20, 4)
            ref = w.at[k, rows_of(rank((0, 3, 1, 2)[j], (0, 3, 1, 2)[i]), 0, SHARD)]
            to = sib
        return remote(ref, ref, w_ss.at[k, m], w_rs.at[k, m], to)

    def w_start(k, *ms):
        for m in ms:
            w_msg(k, m).start()

    def w_recv(k, *ms):
        for m in ms:
            w_msg(k, m).wait_recv()

    def s0(k):
        w_start(k, 0, 1, 4, 5, 20)

    def s1(k):
        w_recv(k, 0)
        w_start(k, 2, 8, 9, 24)
        w_recv(k, 1)
        w_start(k, 3, 12, 13, 28)

    def s2(k):
        w_recv(k, 2, 3)
        w_start(k, 16, 17, 32)

    def s3(k, parts=(0, 1, 2, 3)):
        for j in parts:
            w_recv(k, 4 + 4 * j)
            w_start(k, 6 + 4 * j, 21 + 4 * j)
            w_recv(k, 5 + 4 * j)
            w_start(k, 7 + 4 * j, 22 + 4 * j)

    def s5(k):
        for j in range(4):
            w_recv(k, 6 + 4 * j, 7 + 4 * j)
            w_start(k, 23 + 4 * j)

    def s6(k):
        for m in range(20, 36):
            w_msg(k, m).wait_recv()

    def w_sent(k):
        for m in range(N_MSG):
            w_msg(k, m).wait_send()

    def modulation():
        for base in (0, 4, 8):
            count = 4 if base < 8 else 1
            for k in range(count):
                start = (base + k) * QUART if base < 8 else 2 * WIDTH + x * QUART
                pltpu.make_async_copy(
                    table_ref.at[:, pl.ds(pl.multiple_of(start, 128), QUART)],
                    part.at[k], loc_sem.at[k],
                ).start()
            for k in range(count):
                pltpu.make_async_copy(
                    table_ref.at[:, pl.ds(0, QUART)], part.at[k], loc_sem.at[k]
                ).wait()
                mods[base + k] = jnp.dot(feats_ref[...], part[k], preferred_element_type=F32)
        row = lax.broadcasted_iota(jnp.int32, (16, QUART), 0)
        for q in range(4):
            rows = jnp.where(row < 2, 1.0 + mods[4 + q], jnp.where(row < 4, mods[q], 0.0))
            y[q, ROWS : ROWS + 16] = rows.astype(BF16)

    def block_stats(it, q):
        def body(i, carry):
            rows = pl.ds(pl.multiple_of(32 * i, 32), 32)
            c = cur[it, q, rows].astype(F32)
            mean = jnp.sum(c, axis=-1, keepdims=True) / QUART
            d = c - mean
            stat[q, 0, rows] = jnp.broadcast_to(mean, (32, 128))
            stat[q, 1, rows] = jnp.broadcast_to(jnp.sum(d * d, axis=-1, keepdims=True), (32, 128))
            return carry

        lax.fori_loop(0, 8, body, 0)

    def prepare(q):
        def body(i, carry):
            rows = pl.ds(pl.multiple_of(32 * i, 32), 32)
            p = cur[1, q, rows].astype(F32)
            for step in range(2):
                here = pl.ds(pl.multiple_of(TOK * step + 32 * i, 32), 32)
                c = p if step == 0 else p + tb[q, rows].astype(F32)
                mean = jnp.sum(c, axis=-1, keepdims=True) / QUART
                d = c - mean
                stat[q, 0, here] = jnp.broadcast_to(mean, (32, 128))
                stat[q, 1, here] = jnp.broadcast_to(
                    jnp.sum(d * d, axis=-1, keepdims=True), (32, 128)
                )
                y[q, here] = (d * (1.0 + mods[4 + q, step : step + 1])).astype(BF16)
            return carry

        lax.fori_loop(0, 4, body, 0)

    def block_project(q, cols, first=False):
        rows = pl.ds(pl.multiple_of(q * QUART, 128), QUART)

        def body(k, carry):
            new = jnp.dot(y[q, 0:ROWS], w[k, rows, cols], preferred_element_type=F32)
            acc[k, :, cols] = new if first else acc[k, :, cols] + new
            return carry

        lax.fori_loop(0, 3, body, 0)

    def finalize(c):
        def body(step, i, carry):
            rows = pl.ds(pl.multiple_of(TOK * step + 32 * i, 32), 32)
            means = [stat[q, 0, rows] for q in range(4)]
            mean = (means[0] + means[1] + means[2] + means[3]) * 0.25
            offs = [m - mean for m in means]
            square = jnp.zeros((32, 128), F32)
            for q in range(4):
                square += stat[q, 1, rows] + QUART * offs[q] * offs[q]
            inv = lax.rsqrt(square / WIDTH + 1e-6)
            for k in range(3):
                for h in block_heads[c]:
                    cols = pl.ds(HEAD_SIZE * h, HEAD_SIZE)
                    value = acc[k, rows, cols]
                    add = jnp.zeros((1, HEAD_SIZE), F32)
                    for q in range(4):
                        value += offs[q] * uv[k, q, step : step + 1, cols]
                        add += uv[k, q, 2 + step : 3 + step, cols]
                    qkv[k, rows, cols] = (inv * value + add).astype(BF16)
            return carry

        for step in range(2):
            lax.fori_loop(0, 4, functools.partial(body, step), 0)

    def norm(it):
        def body(i, carry):
            rows = pl.ds(pl.multiple_of(32 * i, 32), 32)
            step = lax.div(i, 4)
            means = [stat[q, 0, rows] for q in range(4)]
            mean = (means[0] + means[1] + means[2] + means[3]) * 0.25
            square = jnp.zeros((32, 128), F32)
            for q in range(4):
                off = means[q] - mean
                square += stat[q, 1, rows] + QUART * off * off
            inv = lax.rsqrt(square / WIDTH + 1e-6)
            for q in range(4):
                for c in range(5):
                    cols = pl.ds(256 * c, 256)
                    m2 = jnp.concatenate([mean, mean], axis=1)
                    i2 = jnp.concatenate([inv, inv], axis=1)
                    d = (cur[it, q, rows, cols].astype(F32) - m2) * i2
                    shift = mods[q, pl.ds(step, 1), cols]
                    scale = mods[4 + q, pl.ds(step, 1), cols]
                    y[q, rows, cols] = (d * (1.0 + scale) + shift).astype(BF16)
            return carry

        lax.fori_loop(0, 8, body, 0)

    def project(k, cols):
        def body(q, carry):
            rows = pl.ds(pl.multiple_of(q * QUART, 128), QUART)
            new = jnp.dot(y[q], w[k, rows, cols], preferred_element_type=F32)
            acc[0, :, cols] += new[:ROWS]
            uv[k, q, :, cols] = new[ROWS:]
            return carry

        acc[0, :, cols] = jnp.zeros((ROWS, cols.size), F32)
        lax.fori_loop(0, 4, body, 0)
        qkv[k, :, cols] = acc[0, :, cols].astype(BF16)

    def attention_block(it, c):
        for step in range(2):
            for n, h in enumerate(block_heads[c]):
                rows, cols = pl.ds(TOK * step, TOK), pl.ds(HEAD_SIZE * h, HEAD_SIZE)
                s = lax.dot_general(
                    qkv[0, rows, cols], qkv[1, rows, cols], (((1,), (1,)), ((), ())),
                    preferred_element_type=F32,
                ) * (1.0 / math.sqrt(HEAD_SIZE))
                e = jnp.exp(s - jnp.max(s, axis=-1, keepdims=True))
                p = (e / jnp.sum(e, axis=-1, keepdims=True)).astype(BF16)
                hd[c][it, x, rows, HEAD_SIZE * n : HEAD_SIZE * (n + 1)] = jnp.dot(
                    p, qkv[2, rows, cols], preferred_element_type=F32
                ).astype(BF16)
        hd_g[it][c].start(0, 1, 2, 3)

    def out_part(it, q, add):
        def body(i, carry):
            rows = pl.ds(pl.multiple_of(q * QUART + i * 256, 128), 256)
            cols = pl.ds(pl.multiple_of(i * 256, 128), 256)
            new = None
            for c in range(2):
                term = lax.dot_general(
                    hd[c][it, q], w[3, rows, blocks[c]], (((1,), (1,)), ((), ())),
                    preferred_element_type=F32,
                )
                new = term if new is None else new + term
            t[:, cols] = t[:, cols] + new if add else new
            return carry

        lax.fori_loop(0, 5, body, 0)

    def out_project(it):
        out_part(it, x, False)
        for g in hd_g[it]:
            g.recv(2)
        out_part(it, x3, True)
        for g in hd_g[it]:
            g.recv(3)
        out_part(it, x1, True)
        for g in hd_g[it]:
            g.recv(4, 5)
        out_part(it, x2, True)

    def hd_sent(it):
        for g in hd_g[it]:
            g.sent()

    first = jnp.where(tm == 0, 1.0, 0.0).astype(F32)

    def terms(it):
        def body(i, carry):
            rows = pl.ds(pl.multiple_of(16 * i, 16), 16)
            step = lax.div(i, 8)
            h = (index_ref[step].astype(F32) + 1.0) / 2000.0
            g = 0.2 * jnp.sqrt(jnp.full((1, 1), h, F32))
            gate = mods[8, pl.ds(step, 1)] * h
            t[rows] = gate * t[rows] + g * nz[rows].astype(F32)
            return carry

        lax.fori_loop(0, 16, body, 0)

        def body2(i, carry):
            rows = pl.ds(pl.multiple_of(16 * i, 16), 16)
            rows1 = pl.ds(pl.multiple_of(TOK + 16 * i, 16), 16)
            t0 = t[rows]
            tf[rows] = t0 + t[rows1] + first * cur[0, x, rows].astype(F32)
            if it == 0:
                tb[x, rows] = t0.astype(BF16)
            return carry

        lax.fori_loop(0, 8, body2, 0)

    mine = pl.ds(pl.multiple_of(64 * core, 64), 64)
    other = pl.ds(pl.multiple_of(64 - 64 * core, 64), 64)
    on0 = jnp.where(is0, 1.0, 0.0).astype(F32)
    on1 = 1.0 - on0

    def px_msg(it, m):
        if m == 0:
            src, dst, to = px_s, px_r.at[it], sib
        elif m == 1:
            src, dst, to = pe_s, pe_r.at[it], sib
        else:
            src, dst, to = sl_s, sl_r, before
        return remote(src, dst, px_ss.at[it, m], px_rs.at[it, m], to)

    starts = (0, 384, 768, 896)

    def piece_msg(it, way, d):
        h = lax.rem(chip + d, 16)
        src, dst = ((p1_s, p1_r), (p2_s, p2_r))[way]
        return remote(
            src.at[h], dst.at[it, chip], a_ss.at[it, way, d], a_rs.at[it, way, d],
            (2 * h + core, x),
        )

    def each(f):
        def body(d, carry):
            f(d)
            return carry

        lax.fori_loop(1, 16, body, 0)

    def prefix(it, idle1, idle2):
        px_s[...] = tf[other].astype(BF16)
        px_msg(it, 0).start()
        if it == ITERS - 1:
            sl_s[...] = t[0:TOK].astype(BF16)
            px_msg(it, 2).start()
        px_msg(it, 0).wait_recv()

        def loop(f):
            def body(i, carry):
                f(i, pl.ds(pl.multiple_of(16 * i, 16), 16),
                  pl.ds(pl.multiple_of(64 * core + 16 * i, 16), 16))
                return carry

            lax.fori_loop(0, 4, body, 0)

        def one(i, r, m):
            v = (tf[m] + px_r[it, r].astype(F32)).astype(BF16)
            for n, at in enumerate(starts):
                p1_s[4 * i + n] = v[:, at : at + 384]

        loop(one)
        each(lambda d: piece_msg(it, 0, d).start())
        p1_r[it, chip] = p1_s[chip]
        idle1()
        each(lambda d: piece_msg(it, 0, d).wait_recv())
        p = jnp.zeros((16, 384), F32)
        for g in range(16):
            p2_s[g] = p.astype(BF16)
            p += p1_r[it, g].astype(F32)
        each(lambda d: piece_msg(it, 1, d).start())
        p2_r[it, chip] = p2_s[chip]
        idle2()
        each(lambda d: piece_msg(it, 0, d).wait_send())
        each(lambda d: piece_msg(it, 1, d).wait_recv())

        def three(i, r, m):
            cut = [p2_r[it, 4 * i + n].astype(F32) for n in range(4)]
            p = jnp.concatenate(cut[:3] + [cut[3][:, 256:]], axis=1)
            pe_s[r] = (p + on0 * tf[m]).astype(BF16)
            p += on1 * px_r[it, r].astype(F32) + first * cur[0, x, m].astype(F32)
            pfx[m] = p
            if it == 0:
                cur[1, x, m] = p.astype(BF16)

        loop(three)
        px_msg(it, 1).start()
        if it == 0:
            pfx_g.start(0)
        each(lambda d: piece_msg(it, 1, d).wait_send())
        px_msg(it, 1).wait_recv()

        def four(i, r, m):
            there = pl.ds(pl.multiple_of(64 - 64 * core + r.start, 16), 16)
            p = pe_r[it, r].astype(F32) + first * cur[0, x, there].astype(F32)
            pfx[there] = p
            if it == 0:
                cur[1, x, there] = p.astype(BF16)

        loop(four)
        if it == 0:
            pfx_g.start(1, 2, 3)
        for m in range(2 + (it == ITERS - 1)):
            px_msg(it, m).wait_send()

    def slide():
        px_msg(ITERS - 1, 2).wait_recv()
        last = tm == 31

        def body(i, carry):
            rows = pl.ds(pl.multiple_of(16 * i, 16), 16)
            rows1 = pl.ds(pl.multiple_of(TOK + 16 * i, 16), 16)
            rows2 = pl.ds(pl.multiple_of(2 * TOK + 16 * i, 16), 16)
            c1 = pfx[rows] + t[rows]
            c2 = c1 + t[rows1]
            c3 = c2 + sl_r[rows].astype(F32)
            c2 = jnp.where(last, c1, c2)
            c3 = jnp.where(last, c1, c3)
            out_ref[rows] = c1.astype(BF16)
            out_ref[rows1] = c2.astype(BF16)
            out_ref[rows2] = c3.astype(BF16)
            return carry

        lax.fori_loop(0, 8, body, 0)

    swap_start()
    lat_g.start(0, 1, 2, 3)
    s0(0)
    s0(1)
    s1(0)
    s2(0)
    s0(2)
    s1(1)
    s2(1)
    lat_g.forward()
    s3(0)
    s1(2)
    s2(2)
    modulation()
    s3(1)
    s5(0)
    swap_finish()
    s0(3)
    block_stats(0, x)
    lat_g.recv(2, 3)
    block_stats(0, x1)
    block_stats(0, x3)
    lat_g.recv(4, 5)
    block_stats(0, x2)
    norm(0)
    s6(0)
    project(0, whole)
    s3(2)
    s5(1)
    s1(3)
    s2(3)
    s6(1)
    project(1, whole)
    s3(3, (0,))
    s5(2)
    s3(3, (1, 2))
    s6(2)
    project(2, blocks[0])
    attention_block(0, 0)
    project(2, blocks[1])
    attention_block(0, 1)
    s3(3, (3,))
    for g in hd_g[0]:
        g.forward()
    s5(3)
    s6(3)
    out_project(0)
    terms(0)
    t0_g.start(0, 1, 2, 3)

    def idle1():
        t0_g.forward()
        lax.fori_loop(0, 2, lambda k, c: (w_sent(k), c)[1], 0)

    def idle2():
        lax.fori_loop(2, 4, lambda k, c: (w_sent(k), c)[1], 0)
        lat_g.sent()
        hd_sent(0)

    def idle3():
        t0_g.sent()
        pfx_g.sent()

    def idle4():
        hd_sent(1)

    prefix(0, idle1, idle2)
    prepare(x)
    pfx_g.forward()
    block_project(x, whole, True)
    t0_g.recv(2, 3, 4, 5)
    pfx_g.recv(2)
    prepare(x3)
    block_project(x3, whole)
    pfx_g.recv(3)
    prepare(x1)
    block_project(x1, whole)
    pfx_g.recv(4, 5)
    prepare(x2)
    block_project(x2, blocks[0])
    finalize(0)
    attention_block(1, 0)
    block_project(x2, blocks[1])
    hd_g[1][0].forward()
    finalize(1)
    attention_block(1, 1)
    hd_g[1][1].forward()
    out_project(1)
    terms(1)
    prefix(1, idle3, idle4)
    slide()


def features(step_index, mod_table):
    half = mod_table.shape[0] // 2
    freqs = jnp.exp(-math.log(10000.0) * jnp.arange(half).astype(F32) / half)
    angles = step_index.astype(F32)[:, None] * freqs[None, :]
    return jnp.concatenate([jnp.cos(angles), jnp.sin(angles)], axis=1).astype(BF16)


def per_device(latents, noise, mod_table, w_query, w_key, w_value, w_out, step_index, slide_offset):
    feats = features(step_index, mod_table)
    feats = jnp.concatenate([feats, feats, jnp.zeros((12, feats.shape[1]), BF16)], axis=0)
    hbm = pl.BlockSpec(memory_space=pl.ANY)
    vmem = pl.BlockSpec(memory_space=pltpu.VMEM)
    smem = pl.BlockSpec(memory_space=pltpu.SMEM)
    dma = pltpu.SemaphoreType.DMA
    out = pl.pallas_call(
        kernel,
        out_shape=jax.ShapeDtypeStruct((3 * TOK, QUART), BF16),
        in_specs=[hbm] * 7 + [vmem, smem],
        out_specs=vmem,
        scratch_shapes=[
            pltpu.VMEM((4, WIDTH, HW), BF16),
            pltpu.VMEM((ITERS, 4, ROWS, QUART), BF16),
            pltpu.VMEM((4, ROWS + 16, QUART), BF16),
            pltpu.VMEM((3, ROWS, HW), F32),
            pltpu.VMEM((3, 4, 16, HW), F32),
            pltpu.VMEM((3, ROWS, HW), BF16),
            pltpu.VMEM((ITERS, 4, ROWS, 256), BF16),
            pltpu.VMEM((ITERS, 4, ROWS, 384), BF16),
            pltpu.VMEM((4, ROWS, QUART), BF16),
            pltpu.VMEM((4, TOK, QUART), BF16),
            pltpu.VMEM((ROWS, QUART), F32),
            pltpu.VMEM((ROWS, QUART), BF16),
            pltpu.VMEM((9, 16, QUART), F32),
            pltpu.VMEM((4, 2, ROWS, 128), F32),
            pltpu.VMEM((TOK, QUART), F32),
            pltpu.VMEM((64, QUART), BF16),
            pltpu.VMEM((ITERS, 64, QUART), BF16),
            pltpu.VMEM((16, 16, 384), BF16),
            pltpu.VMEM((ITERS, 16, 16, 384), BF16),
            pltpu.VMEM((16, 16, 384), BF16),
            pltpu.VMEM((ITERS, 16, 16, 384), BF16),
            pltpu.VMEM((64, QUART), BF16),
            pltpu.VMEM((ITERS, 64, QUART), BF16),
            pltpu.VMEM((TOK, QUART), F32),
            pltpu.VMEM((TOK, QUART), BF16),
            pltpu.VMEM((TOK, QUART), BF16),
            dma((7,)),
            dma((4, N_MSG)),
            dma((4, N_MSG)),
            dma((3, 6)),
            dma((3, 6)),
            dma((ITERS, 2, 6)),
            dma((ITERS, 2, 6)),
            dma((ITERS, 3)),
            dma((ITERS, 3)),
            dma((ITERS, 2, 16)),
            dma((ITERS, 2, 16)),
            dma,
            dma,
        ],
        compiler_params=pltpu.CompilerParams(
            collective_id=0, has_side_effects=True, vmem_limit_bytes=62 * 1024 * 1024
        ),
        cost_estimate=pl.CostEstimate(
            flops=2 * ITERS * 4 * ROWS * WIDTH * HW, bytes_accessed=12_000_000, transcendentals=0
        ),
    )(
        latents.reshape(ROWS, QUART), noise.reshape(ROWS, QUART), mod_table,
        w_query, w_key, w_value, w_out.T, feats, step_index,
    )
    return lax.dynamic_slice_in_dim(out.reshape(3, TOK, QUART), slide_offset - 1, 2, 0)


def solution(mesh):
    placed = (
        P("tm", None, "tp"),
        P("tm", None, "tp"),
        P(),
        P("tm", "tp"),
        P("tm", "tp"),
        P("tm", "tp"),
        P("tp", "tm"),
        P("tm"),
        P(),
    )
    return jax.shard_map(
        per_device, mesh=mesh, in_specs=placed, out_specs=P("tm", None, "tp"), check_vma=False
    )
```

```python
import functools
import math

import jax
import jax.numpy as jnp
from jax import lax
from jax.experimental import pallas as pl
from jax.experimental.pallas import tpu as pltpu
from jax.sharding import PartitionSpec as P

HEAD_SIZE = 128
HEADS = 5
ITERS = 2
TOK = 128
ROWS = 256
QUART = 1280
WIDTH = 5120
HW = 640
SHARD = 160
HALF = 80
MESH = pl.DeviceIdType.MESH
F32 = jnp.float32
BF16 = jnp.bfloat16
N_MSG = 36


def kernel(
    lat_ref, noise_ref, table_ref, wq_ref, wk_ref, wv_ref, wo_ref, feats_ref, index_ref,
    out_ref,
    w, cur, y, acc, uv, qkv, hda, hdb, part, tb, t, nz, mods, stat,
    tf, px_s, px_r, p1_s, p1_r, p2_s, p2_r, pe_s, pe_r, pfx, sl_s, sl_r,
    loc_sem, w_ss, w_rs, ag_ss, ag_rs, hd_ss, hd_rs, px_ss, px_rs, a_ss, a_rs, tr_ss, tr_rs,
):
    tm = lax.axis_index("tm")
    x = lax.axis_index("tp")
    core = lax.rem(tm, 2)
    chip = lax.div(tm, 2)
    yy, zz = lax.div(chip, 4), lax.rem(chip, 4)
    is0 = core == 0
    a = jnp.where(is0, zz, yy)
    b = jnp.where(is0, yy, zz)

    def rank(da, db):
        aa, bb = lax.rem(a + da, 4), lax.rem(b + db, 4)
        return jnp.where(is0, bb * 4 + aa, aa * 4 + bb) * 2 + core

    def dev(da, db):
        return (rank(da, db), x)

    sib = (tm + 1 - 2 * core, x)
    xp = (tm, lax.rem(x + 1, 4))
    xm = (tm, lax.rem(x + 3, 4))
    following = (lax.rem(tm + 1, 32), x)
    before = (lax.rem(tm + 31, 32), x)
    swapped = ((x * 4 + zz) * 2 + core, yy)
    swaps = x != yy
    x1, x2, x3 = lax.rem(x + 1, 4), lax.rem(x + 2, 4), lax.rem(x + 3, 4)

    def remote(src, dst, ss, rs, to):
        return pltpu.make_async_remote_copy(
            src_ref=src, dst_ref=dst, send_sem=ss, recv_sem=rs, device_id=to, device_id_type=MESH
        )

    own = pl.ds(pl.multiple_of(SHARD * tm, 16), SHARD)
    local = [
        pltpu.make_async_copy(src, w.at[k, own], loc_sem.at[k])
        for k, src in enumerate((wq_ref, wk_ref, wv_ref))
    ]
    local.append(pltpu.make_async_copy(lat_ref, cur.at[0, x], loc_sem.at[4]))
    local.append(pltpu.make_async_copy(noise_ref, nz, loc_sem.at[5]))
    for c in local:
        c.start()

    barrier = pltpu.get_barrier_semaphore()
    peers = [sib, xp, xm, following, before]
    peers += [(2 * lax.rem(chip + d, 16) + core, x) for d in range(1, 16)]
    for peer in peers:
        pl.semaphore_signal(barrier, inc=1, device_id=peer, device_id_type=MESH)

    @pl.when(swaps)
    def _():
        pl.semaphore_signal(barrier, inc=1, device_id=swapped, device_id_type=MESH)

    pl.semaphore_wait(barrier, len(peers) + jnp.where(swaps, 1, 0))

    def swap_msg():
        there = pl.ds(pl.multiple_of(SHARD * swapped[0], 16), SHARD)
        return remote(wo_ref, w.at[3, there], tr_ss, tr_rs, swapped)

    def swap_local():
        return pltpu.make_async_copy(wo_ref, w.at[3, own], loc_sem.at[6])

    def swap_start():
        @pl.when(swaps)
        def _():
            swap_msg().start()

        @pl.when(jnp.logical_not(swaps))
        def _():
            swap_local().start()

    def swap_finish():
        @pl.when(swaps)
        def _():
            swap_msg().wait()

        @pl.when(jnp.logical_not(swaps))
        def _():
            swap_local().wait()

    for c in local:
        c.wait()

    class Gather:
        def __init__(self, block, halves, ss, rs):
            self.block, self.halves, self.ss, self.rs = block, halves, ss, rs

        def msg(self, m):
            to = xp if m in (0, 2, 4) else xm
            src = (x, x, x, x, x3, x1)[m]
            ref = self.block(src, self.halves[(0, 1, 1, 0, 0, 1)[m]])
            return remote(ref, ref, self.ss(m), self.rs(m), to)

        def start(self, *ms):
            for m in ms:
                self.msg(m).start()

        def forward(self):
            self.msg(0).wait_recv()
            self.msg(4).start()
            self.msg(1).wait_recv()
            self.msg(5).start()

        def recv(self, *ms):
            for m in ms:
                self.msg(m).wait_recv()

        def sent(self):
            for m in range(6):
                self.msg(m).wait_send()

    steps = (pl.ds(0, TOK), pl.ds(TOK, TOK))
    lat_g = Gather(lambda q, r: cur.at[0, q, r], steps, lambda m: ag_ss.at[0, m], lambda m: ag_rs.at[0, m])
    t0_g = Gather(
        lambda q, r: tb.at[q, r], (pl.ds(0, 64), pl.ds(64, 64)),
        lambda m: ag_ss.at[1, m], lambda m: ag_rs.at[1, m],
    )
    pfx_g = Gather(
        lambda q, r: cur.at[1, q, r],
        (pl.ds(pl.multiple_of(64 * core, 64), 64), pl.ds(pl.multiple_of(64 - 64 * core, 64), 64)),
        lambda m: ag_ss.at[2, m], lambda m: ag_rs.at[2, m],
    )
    hd = (hda, hdb)
    blocks = (pl.ds(0, 256), pl.ds(256, 384))
    block_heads = ((0, 1), (2, 3, 4))
    whole = pl.ds(0, HW)

    def hd_gather(it, c):
        return Gather(
            lambda q, r: hd[c].at[it, q, r], steps,
            lambda m: hd_ss.at[it, c, m], lambda m: hd_rs.at[it, c, m],
        )

    hd_g = [[hd_gather(it, c) for c in range(2)] for it in range(ITERS)]

    def rows_of(r, lo, n):
        return pl.ds(pl.multiple_of(SHARD * r + lo, 16), n)

    def w_msg(k, m):
        if m < 4:
            ref = (
                w.at[k, rows_of(tm, 0, SHARD)],
                w.at[k, rows_of(tm, 0, SHARD)],
                w.at[k, rows_of(rank(3, 0), 0, HALF)],
                w.at[k, rows_of(rank(1, 0), HALF, HALF)],
            )[m]
            to = dev(1, 0) if m in (0, 2) else dev(3, 0)
        elif m < 20:
            j, i = divmod(m - 4, 4)
            da = (0, 3, 1, 2)[j]
            ref = (
                w.at[k, rows_of(rank(da, 0), 0, SHARD)],
                w.at[k, rows_of(rank(da, 0), 0, SHARD)],
                w.at[k, rows_of(rank(da, 3), 0, HALF)],
                w.at[k, rows_of(rank(da, 1), HALF, HALF)],
            )[i]
            to = dev(0, 1) if i in (0, 2) else dev(0, 3)
        else:
            j, i = divmod(m - 20, 4)
            ref = w.at[k, rows_of(rank((0, 3, 1, 2)[j], (0, 3, 1, 2)[i]), 0, SHARD)]
            to = sib
        return remote(ref, ref, w_ss.at[k, m], w_rs.at[k, m], to)

    def w_start(k, *ms):
        for m in ms:
            w_msg(k, m).start()

    def w_recv(k, *ms):
        for m in ms:
            w_msg(k, m).wait_recv()

    def s0(k):
        w_start(k, 0, 1, 4, 5, 20)

    def s1(k):
        w_recv(k, 0)
        w_start(k, 2, 8, 9, 24)
        w_recv(k, 1)
        w_start(k, 3, 12, 13, 28)

    def s2(k):
        w_recv(k, 2, 3)
        w_start(k, 16, 17, 32)

    def s3(k, parts=(0, 1, 2, 3)):
        for j in parts:
            w_recv(k, 4 + 4 * j)
            w_start(k, 6 + 4 * j, 21 + 4 * j)
            w_recv(k, 5 + 4 * j)
            w_start(k, 7 + 4 * j, 22 + 4 * j)

    def s5(k):
        for j in range(4):
            w_recv(k, 6 + 4 * j, 7 + 4 * j)
            w_start(k, 23 + 4 * j)

    def s6(k):
        for m in range(20, 36):
            w_msg(k, m).wait_recv()

    def w_sent(k):
        for m in range(N_MSG):
            w_msg(k, m).wait_send()

    def modulation():
        for base in (0, 4, 8):
            count = 4 if base < 8 else 1
            for k in range(count):
                start = (base + k) * QUART if base < 8 else 2 * WIDTH + x * QUART
                pltpu.make_async_copy(
                    table_ref.at[:, pl.ds(pl.multiple_of(start, 128), QUART)],
                    part.at[k], loc_sem.at[k],
                ).start()
            for k in range(count):
                pltpu.make_async_copy(
                    table_ref.at[:, pl.ds(0, QUART)], part.at[k], loc_sem.at[k]
                ).wait()
                mods[base + k] = jnp.dot(feats_ref[...], part[k], preferred_element_type=F32)
        row = lax.broadcasted_iota(jnp.int32, (16, QUART), 0)
        for q in range(4):
            rows = jnp.where(row < 2, 1.0 + mods[4 + q], jnp.where(row < 4, mods[q], 0.0))
            y[q, ROWS : ROWS + 16] = rows.astype(BF16)

    def block_stats(it, q):
        def body(i, carry):
            rows = pl.ds(pl.multiple_of(32 * i, 32), 32)
            c = cur[it, q, rows].astype(F32)
            mean = jnp.sum(c, axis=-1, keepdims=True) / QUART
            d = c - mean
            stat[q, 0, rows] = jnp.broadcast_to(mean, (32, 128))
            stat[q, 1, rows] = jnp.broadcast_to(jnp.sum(d * d, axis=-1, keepdims=True), (32, 128))
            return carry

        lax.fori_loop(0, 8, body, 0)

    def prepare(q):
        def body(i, carry):
            rows = pl.ds(pl.multiple_of(32 * i, 32), 32)
            p = cur[1, q, rows].astype(F32)
            for step in range(2):
                here = pl.ds(pl.multiple_of(TOK * step + 32 * i, 32), 32)
                c = p if step == 0 else p + tb[q, rows].astype(F32)
                mean = jnp.sum(c, axis=-1, keepdims=True) / QUART
                d = c - mean
                stat[q, 0, here] = jnp.broadcast_to(mean, (32, 128))
                stat[q, 1, here] = jnp.broadcast_to(
                    jnp.sum(d * d, axis=-1, keepdims=True), (32, 128)
                )
                y[q, here] = (d * (1.0 + mods[4 + q, step : step + 1])).astype(BF16)
            return carry

        lax.fori_loop(0, 4, body, 0)

    def block_project(q, cols, first=False):
        rows = pl.ds(pl.multiple_of(q * QUART, 128), QUART)

        def body(k, carry):
            new = jnp.dot(y[q, 0:ROWS], w[k, rows, cols], preferred_element_type=F32)
            acc[k, :, cols] = new if first else acc[k, :, cols] + new
            return carry

        lax.fori_loop(0, 3, body, 0)

    def finalize(c):
        def body(step, i, carry):
            rows = pl.ds(pl.multiple_of(TOK * step + 32 * i, 32), 32)
            means = [stat[q, 0, rows] for q in range(4)]
            mean = (means[0] + means[1] + means[2] + means[3]) * 0.25
            offs = [m - mean for m in means]
            square = jnp.zeros((32, 128), F32)
            for q in range(4):
                square += stat[q, 1, rows] + QUART * offs[q] * offs[q]
            inv = lax.rsqrt(square / WIDTH + 1e-6)
            for k in range(3):
                for h in block_heads[c]:
                    cols = pl.ds(HEAD_SIZE * h, HEAD_SIZE)
                    value = acc[k, rows, cols]
                    add = jnp.zeros((1, HEAD_SIZE), F32)
                    for q in range(4):
                        value += offs[q] * uv[k, q, step : step + 1, cols]
                        add += uv[k, q, 2 + step : 3 + step, cols]
                    qkv[k, rows, cols] = (inv * value + add).astype(BF16)
            return carry

        for step in range(2):
            lax.fori_loop(0, 4, functools.partial(body, step), 0)

    def norm(it):
        def body(i, carry):
            rows = pl.ds(pl.multiple_of(32 * i, 32), 32)
            step = lax.div(i, 4)
            means = [stat[q, 0, rows] for q in range(4)]
            mean = (means[0] + means[1] + means[2] + means[3]) * 0.25
            square = jnp.zeros((32, 128), F32)
            for q in range(4):
                off = means[q] - mean
                square += stat[q, 1, rows] + QUART * off * off
            inv = lax.rsqrt(square / WIDTH + 1e-6)
            for q in range(4):
                for c in range(5):
                    cols = pl.ds(256 * c, 256)
                    m2 = jnp.concatenate([mean, mean], axis=1)
                    i2 = jnp.concatenate([inv, inv], axis=1)
                    d = (cur[it, q, rows, cols].astype(F32) - m2) * i2
                    shift = mods[q, pl.ds(step, 1), cols]
                    scale = mods[4 + q, pl.ds(step, 1), cols]
                    y[q, rows, cols] = (d * (1.0 + scale) + shift).astype(BF16)
            return carry

        lax.fori_loop(0, 8, body, 0)

    def project(k, cols):
        def body(q, carry):
            rows = pl.ds(pl.multiple_of(q * QUART, 128), QUART)
            new = jnp.dot(y[q], w[k, rows, cols], preferred_element_type=F32)
            acc[0, :, cols] += new[:ROWS]
            uv[k, q, :, cols] = new[ROWS:]
            return carry

        acc[0, :, cols] = jnp.zeros((ROWS, cols.size), F32)
        lax.fori_loop(0, 4, body, 0)
        qkv[k, :, cols] = acc[0, :, cols].astype(BF16)

    def attention_block(it, c):
        for step in range(2):
            for n, h in enumerate(block_heads[c]):
                rows, cols = pl.ds(TOK * step, TOK), pl.ds(HEAD_SIZE * h, HEAD_SIZE)
                s = lax.dot_general(
                    qkv[0, rows, cols], qkv[1, rows, cols], (((1,), (1,)), ((), ())),
                    preferred_element_type=F32,
                ) * (1.0 / math.sqrt(HEAD_SIZE))
                e = jnp.exp(s - jnp.max(s, axis=-1, keepdims=True))
                p = (e / jnp.sum(e, axis=-1, keepdims=True)).astype(BF16)
                hd[c][it, x, rows, HEAD_SIZE * n : HEAD_SIZE * (n + 1)] = jnp.dot(
                    p, qkv[2, rows, cols], preferred_element_type=F32
                ).astype(BF16)
        hd_g[it][c].start(0, 1, 2, 3)

    def out_part(it, q, add):
        def body(i, carry):
            rows = pl.ds(pl.multiple_of(q * QUART + i * 256, 128), 256)
            cols = pl.ds(pl.multiple_of(i * 256, 128), 256)
            new = None
            for c in range(2):
                term = lax.dot_general(
                    hd[c][it, q], w[3, rows, blocks[c]], (((1,), (1,)), ((), ())),
                    preferred_element_type=F32,
                )
                new = term if new is None else new + term
            t[:, cols] = t[:, cols] + new if add else new
            return carry

        lax.fori_loop(0, 5, body, 0)

    def out_project(it):
        out_part(it, x, False)
        for g in hd_g[it]:
            g.recv(2)
        out_part(it, x3, True)
        for g in hd_g[it]:
            g.recv(3)
        out_part(it, x1, True)
        for g in hd_g[it]:
            g.recv(4, 5)
        out_part(it, x2, True)

    def hd_sent(it):
        for g in hd_g[it]:
            g.sent()

    first = jnp.where(tm == 0, 1.0, 0.0).astype(F32)

    def terms(it):
        def body(i, carry):
            rows = pl.ds(pl.multiple_of(16 * i, 16), 16)
            step = lax.div(i, 8)
            h = (index_ref[step].astype(F32) + 1.0) / 2000.0
            g = 0.2 * jnp.sqrt(jnp.full((1, 1), h, F32))
            gate = mods[8, pl.ds(step, 1)] * h
            t[rows] = gate * t[rows] + g * nz[rows].astype(F32)
            return carry

        lax.fori_loop(0, 16, body, 0)

        def body2(i, carry):
            rows = pl.ds(pl.multiple_of(16 * i, 16), 16)
            rows1 = pl.ds(pl.multiple_of(TOK + 16 * i, 16), 16)
            t0 = t[rows]
            tf[rows] = t0 + t[rows1] + first * cur[0, x, rows].astype(F32)
            if it == 0:
                tb[x, rows] = t0.astype(BF16)
            return carry

        lax.fori_loop(0, 8, body2, 0)

    mine = pl.ds(pl.multiple_of(64 * core, 64), 64)
    other = pl.ds(pl.multiple_of(64 - 64 * core, 64), 64)
    on0 = jnp.where(is0, 1.0, 0.0).astype(F32)
    on1 = 1.0 - on0

    def px_msg(it, m):
        if m == 0:
            src, dst, to = px_s, px_r.at[it], sib
        elif m == 1:
            src, dst, to = pe_s, pe_r.at[it], sib
        else:
            src, dst, to = sl_s, sl_r, before
        return remote(src, dst, px_ss.at[it, m], px_rs.at[it, m], to)

    starts = (0, 384, 768, 896)

    def piece_msg(it, way, d):
        h = lax.rem(chip + d, 16)
        src, dst = ((p1_s, p1_r), (p2_s, p2_r))[way]
        return remote(
            src.at[h], dst.at[it, chip], a_ss.at[it, way, d], a_rs.at[it, way, d],
            (2 * h + core, x),
        )

    def each(f):
        def body(i, carry):
            for n in (1, 2, 3):
                f(3 * i + n)
            return carry

        lax.fori_loop(0, 5, body, 0)

    def prefix(it, idle1, idle2):
        px_s[...] = tf[other].astype(BF16)
        px_msg(it, 0).start()
        if it == ITERS - 1:
            sl_s[...] = t[0:TOK].astype(BF16)
            px_msg(it, 2).start()
        px_msg(it, 0).wait_recv()

        def loop(f):
            def body(i, carry):
                f(i, pl.ds(pl.multiple_of(16 * i, 16), 16),
                  pl.ds(pl.multiple_of(64 * core + 16 * i, 16), 16))
                return carry

            lax.fori_loop(0, 4, body, 0)

        def one(i, r, m):
            v = (tf[m] + px_r[it, r].astype(F32)).astype(BF16)
            for n, at in enumerate(starts):
                p1_s[4 * i + n] = v[:, at : at + 384]

        loop(one)
        each(lambda d: piece_msg(it, 0, d).start())
        p1_r[it, chip] = p1_s[chip]
        idle1()
        each(lambda d: piece_msg(it, 0, d).wait_recv())
        p = jnp.zeros((16, 384), F32)
        for g in range(16):
            p2_s[g] = p.astype(BF16)
            p += p1_r[it, g].astype(F32)
        each(lambda d: piece_msg(it, 1, d).start())
        p2_r[it, chip] = p2_s[chip]
        idle2()
        each(lambda d: piece_msg(it, 0, d).wait_send())
        each(lambda d: piece_msg(it, 1, d).wait_recv())

        def three(i, r, m):
            cut = [p2_r[it, 4 * i + n].astype(F32) for n in range(4)]
            p = jnp.concatenate(cut[:3] + [cut[3][:, 256:]], axis=1)
            pe_s[r] = (p + on0 * tf[m]).astype(BF16)
            p += on1 * px_r[it, r].astype(F32) + first * cur[0, x, m].astype(F32)
            pfx[m] = p
            if it == 0:
                cur[1, x, m] = p.astype(BF16)

        loop(three)
        px_msg(it, 1).start()
        if it == 0:
            pfx_g.start(0)
        each(lambda d: piece_msg(it, 1, d).wait_send())
        px_msg(it, 1).wait_recv()

        def four(i, r, m):
            there = pl.ds(pl.multiple_of(64 - 64 * core + r.start, 16), 16)
            p = pe_r[it, r].astype(F32) + first * cur[0, x, there].astype(F32)
            pfx[there] = p
            if it == 0:
                cur[1, x, there] = p.astype(BF16)

        loop(four)
        if it == 0:
            pfx_g.start(1, 2, 3)
        for m in range(2 + (it == ITERS - 1)):
            px_msg(it, m).wait_send()

    def slide():
        px_msg(ITERS - 1, 2).wait_recv()
        last = tm == 31

        def body(i, carry):
            rows = pl.ds(pl.multiple_of(16 * i, 16), 16)
            rows1 = pl.ds(pl.multiple_of(TOK + 16 * i, 16), 16)
            rows2 = pl.ds(pl.multiple_of(2 * TOK + 16 * i, 16), 16)
            c1 = pfx[rows] + t[rows]
            c2 = c1 + t[rows1]
            c3 = c2 + sl_r[rows].astype(F32)
            c2 = jnp.where(last, c1, c2)
            c3 = jnp.where(last, c1, c3)
            out_ref[rows] = c1.astype(BF16)
            out_ref[rows1] = c2.astype(BF16)
            out_ref[rows2] = c3.astype(BF16)
            return carry

        lax.fori_loop(0, 8, body, 0)

    swap_start()
    lat_g.start(0, 1, 2, 3)
    s0(0)
    s0(1)
    s1(0)
    s2(0)
    s0(2)
    s1(1)
    s2(1)
    lat_g.forward()
    s3(0)
    s1(2)
    s2(2)
    modulation()
    s3(1)
    s5(0)
    swap_finish()
    s0(3)
    block_stats(0, x)
    lat_g.recv(2, 3)
    block_stats(0, x1)
    block_stats(0, x3)
    lat_g.recv(4, 5)
    block_stats(0, x2)
    norm(0)
    s6(0)
    project(0, whole)
    s3(2)
    s5(1)
    s1(3)
    s2(3)
    s6(1)
    project(1, whole)
    s3(3, (0,))
    s5(2)
    s3(3, (1, 2))
    s6(2)
    project(2, blocks[0])
    attention_block(0, 0)
    project(2, blocks[1])
    attention_block(0, 1)
    s3(3, (3,))
    for g in hd_g[0]:
        g.forward()
    s5(3)
    s6(3)
    out_project(0)
    terms(0)
    t0_g.start(0, 1, 2, 3)

    def idle1():
        t0_g.forward()
        lax.fori_loop(0, 2, lambda k, c: (w_sent(k), c)[1], 0)

    def idle2():
        lax.fori_loop(2, 4, lambda k, c: (w_sent(k), c)[1], 0)
        lat_g.sent()
        hd_sent(0)

    def idle3():
        t0_g.sent()
        pfx_g.sent()

    def idle4():
        hd_sent(1)

    prefix(0, idle1, idle2)
    prepare(x)
    pfx_g.forward()
    block_project(x, whole, True)
    t0_g.recv(2, 3, 4, 5)
    pfx_g.recv(2)
    prepare(x3)
    block_project(x3, whole)
    pfx_g.recv(3)
    prepare(x1)
    block_project(x1, whole)
    pfx_g.recv(4, 5)
    prepare(x2)
    block_project(x2, blocks[0])
    finalize(0)
    attention_block(1, 0)
    block_project(x2, blocks[1])
    hd_g[1][0].forward()
    finalize(1)
    attention_block(1, 1)
    hd_g[1][1].forward()
    out_project(1)
    terms(1)
    prefix(1, idle3, idle4)
    slide()


def features(step_index, mod_table):
    half = mod_table.shape[0] // 2
    freqs = jnp.exp(-math.log(10000.0) * jnp.arange(half).astype(F32) / half)
    angles = step_index.astype(F32)[:, None] * freqs[None, :]
    return jnp.concatenate([jnp.cos(angles), jnp.sin(angles)], axis=1).astype(BF16)


def per_device(latents, noise, mod_table, w_query, w_key, w_value, w_out, step_index, slide_offset):
    feats = features(step_index, mod_table)
    feats = jnp.concatenate([feats, feats, jnp.zeros((12, feats.shape[1]), BF16)], axis=0)
    hbm = pl.BlockSpec(memory_space=pl.ANY)
    vmem = pl.BlockSpec(memory_space=pltpu.VMEM)
    smem = pl.BlockSpec(memory_space=pltpu.SMEM)
    dma = pltpu.SemaphoreType.DMA
    out = pl.pallas_call(
        kernel,
        out_shape=jax.ShapeDtypeStruct((3 * TOK, QUART), BF16),
        in_specs=[hbm] * 7 + [vmem, smem],
        out_specs=vmem,
        scratch_shapes=[
            pltpu.VMEM((4, WIDTH, HW), BF16),
            pltpu.VMEM((ITERS, 4, ROWS, QUART), BF16),
            pltpu.VMEM((4, ROWS + 16, QUART), BF16),
            pltpu.VMEM((3, ROWS, HW), F32),
            pltpu.VMEM((3, 4, 16, HW), F32),
            pltpu.VMEM((3, ROWS, HW), BF16),
            pltpu.VMEM((ITERS, 4, ROWS, 256), BF16),
            pltpu.VMEM((ITERS, 4, ROWS, 384), BF16),
            pltpu.VMEM((4, ROWS, QUART), BF16),
            pltpu.VMEM((4, TOK, QUART), BF16),
            pltpu.VMEM((ROWS, QUART), F32),
            pltpu.VMEM((ROWS, QUART), BF16),
            pltpu.VMEM((9, 16, QUART), F32),
            pltpu.VMEM((4, 2, ROWS, 128), F32),
            pltpu.VMEM((TOK, QUART), F32),
            pltpu.VMEM((64, QUART), BF16),
            pltpu.VMEM((ITERS, 64, QUART), BF16),
            pltpu.VMEM((16, 16, 384), BF16),
            pltpu.VMEM((ITERS, 16, 16, 384), BF16),
            pltpu.VMEM((16, 16, 384), BF16),
            pltpu.VMEM((ITERS, 16, 16, 384), BF16),
            pltpu.VMEM((64, QUART), BF16),
            pltpu.VMEM((ITERS, 64, QUART), BF16),
            pltpu.VMEM((TOK, QUART), F32),
            pltpu.VMEM((TOK, QUART), BF16),
            pltpu.VMEM((TOK, QUART), BF16),
            dma((7,)),
            dma((4, N_MSG)),
            dma((4, N_MSG)),
            dma((3, 6)),
            dma((3, 6)),
            dma((ITERS, 2, 6)),
            dma((ITERS, 2, 6)),
            dma((ITERS, 3)),
            dma((ITERS, 3)),
            dma((ITERS, 2, 16)),
            dma((ITERS, 2, 16)),
            dma,
            dma,
        ],
        compiler_params=pltpu.CompilerParams(
            collective_id=0, has_side_effects=True, vmem_limit_bytes=62 * 1024 * 1024
        ),
        cost_estimate=pl.CostEstimate(
            flops=2 * ITERS * 4 * ROWS * WIDTH * HW, bytes_accessed=12_000_000, transcendentals=0
        ),
    )(
        latents.reshape(ROWS, QUART), noise.reshape(ROWS, QUART), mod_table,
        w_query, w_key, w_value, w_out.T, feats, step_index,
    )
    return lax.dynamic_slice_in_dim(out.reshape(3, TOK, QUART), slide_offset - 1, 2, 0)


def solution(mesh):
    placed = (
        P("tm", None, "tp"),
        P("tm", None, "tp"),
        P(),
        P("tm", "tp"),
        P("tm", "tp"),
        P("tm", "tp"),
        P("tp", "tm"),
        P("tm"),
        P(),
    )
    return jax.shard_map(
        per_device, mesh=mesh, in_specs=placed, out_specs=P("tm", None, "tp"), check_vma=False
    )
```
